128 devices in a mesh: expert: 64 (over z, y, x), edata: 2 (over core).
Axes of the slice: x: 4, y: 4, z: 4, core: 2. Of those that a mesh axis runs over, the one named last changes fastest.
Arguments:
- tokens: bfloat16 [16384, 2048], P(('expert', 'edata')), may hold values from -6 to 6
- cotangent: bfloat16 [16384, 2048], P(('expert', 'edata')), may hold values from -4 to 4
- expert_ids: int32 [16384, 8], P(('expert', 'edata')), may hold values from 0 to 63, all different within a row; in each aligned block of 128 rows (0 to 127, 128 to 255, ...) at most 24 rows name the same one
- gates: float32 [16384, 8], P(('expert', 'edata')), may hold values from 0.05 to 0.5
- w_gate: bfloat16 [64, 2048, 384], P('expert'), may hold values from -0.125 to 0.125
- w_up: bfloat16 [64, 2048, 384], P('expert'), may hold values from -0.125 to 0.125
- w_down: bfloat16 [64, 384, 2048], P('expert'), may hold values from -0.3125 to 0.3125
Outputs:
- mixed: bfloat16 [16384, 2048], P(('expert', 'edata'))
- input_grad: bfloat16 [16384, 2048], P(('expert', 'edata'))
- grad_gate: float32 [64, 2048, 384], P('expert', 'edata')
- grad_up: float32 [64, 2048, 384], P('expert', 'edata')
- grad_down: float32 [64, 384, 2048], P('expert', None, 'edata')
The draws below stay inside these ranges and needn't reach their ends.
Inputs may be any that keep to these rules, and one draw needn't show every extreme that they name: `expert_ids`: each token names 8 different experts. Among the rows of one device no expert is named more than 24 times, and in every draw some device names some expert exactly 24 times.
All inputs are finite; a program needn't handle non-finite values.
Results may differ from the reference program's by a relative error of at most 0.0064.
Values may be sent and summed in bfloat16 or wider, within the bound.
No kernel may reach another device: no remote copies, remote signals or barrier semaphores. Data moves between devices by JAX's collectives and lax.ppermute only.
A program may use at most 128 MiB of HBM per device.

```python
import math
from functools import partial
import jax
import jax.numpy as jnp
import numpy as np
from jax import lax

D = 2048
H = 384
TOP = 8
TOK_DEV = 128
EXPERTS = 64
CAP = 24
TOKENS = 16384


def steps_of(rng, shape, pieces, least, top_value):
    gain = 1.0
    for dim, parts in pieces:
        draws = jax.random.uniform(jax.random.fold_in(jax.random.fold_in(rng, 6), dim), (parts,), jnp.float32, least / len(pieces), top_value / len(pieces))
        gain = gain * jnp.repeat(jnp.exp(draws), shape[dim] // parts).reshape((-1,) + (1,) * (len(shape) - 1 - dim))
    return gain


def deal_out(stream_key, own, number, rows, count, top, most, skew):
    ranking = jax.random.permutation(stream_key, count)
    packed, ordinary = shares(count, rows * top, most, skew, True), shares(count, rows * top, most, skew, False)
    places = jnp.arange(count)

    def named(sizes, offset_by):
        used = int((sizes > 0).sum())
        fixed = max(1, used // 4)
        passed = fixed + (places - fixed + offset_by * (used - fixed)) % max(1, count - fixed)
        return jnp.zeros((count,), jnp.int32).at[ranking[jnp.where(places < fixed, places, passed)]].set(jnp.asarray(sizes, jnp.int32))

    sizes = jnp.where(number % 4 == 0, named(packed, number // 4), named(ordinary, number - number // 4 - 1))
    mixed = jax.random.permutation(jax.random.fold_in(own, 3), count)
    giver, sink = mixed[0:count // 2 * 2:2], mixed[1:count // 2 * 2:2]
    margin = jnp.minimum(sizes[giver] - 1, most - sizes[sink]) // 2
    margin = jnp.where((giver == ranking[0]) | (sink == ranking[0]) | (sizes[sink] == 0), 0, jnp.maximum(margin, 0))
    passed = jax.random.randint(jax.random.fold_in(own, 4), (count // 2,), 0, 1 << 20) % (margin + 1)
    sizes = sizes.at[giver].add(-passed).at[sink].add(passed)
    items = jnp.searchsorted(jnp.cumsum(sizes), jnp.arange(rows * top), side="right").astype(jnp.int32)
    grid = items.reshape(top, rows).T
    grid = grid[jax.random.permutation(jax.random.fold_in(own, 1), rows)]
    offset_by = jax.random.randint(jax.random.fold_in(own, 2), (rows, 1), 0, top)
    return jnp.take_along_axis(grid, (jnp.arange(top)[None, :] + offset_by) % top, axis=1)


def shares(amount, total, bound, lean, full):
    loads = [(1 << 20) // math.isqrt(rank ** lean) + 1 for rank in range(1, amount + 1)]
    largest = bound if full else min(bound, max(-(-total // amount), total * loads[0] // sum(loads)))
    least = 1 if total - largest >= amount - 1 else 0
    given, rest = [largest] + [least] * (amount - 1), total - largest - least * (amount - 1)
    while rest > 0:
        free = [i for i in range(1, amount) if given[i] < largest] or [i for i in range(1, amount) if given[i] < bound]
        pool, left = sum([loads[i] for i in free]), rest
        for i in free:
            more = min(bound - given[i], max(1, left * loads[i] // pool), rest)
            given[i] = given[i] + more
            rest = rest - more
    return np.array(given)


def noise(key, shape, scale, bound, split=(), held_as=jnp.bfloat16):
    entries = scale * jax.random.normal(key, shape, jnp.float32)
    if split:
        entries = entries * steps_of(key, shape, split, -0.22, 0.18)
    return jnp.clip(entries, -bound, bound).astype(held_as)


def setup_inputs(seed: int = 0) -> dict:
    streams_of = jax.random.split(jax.random.key(seed), 8)
    tokens = noise(streams_of[0], (TOKENS, D), 1.0, 6.0, ((0, 128),))
    cotangent = noise(streams_of[1], (TOKENS, D), 0.5, 4.0, ((0, 128),))
    expert_ids_keys = jax.random.split(jax.random.fold_in(streams_of[2], 1), TOKENS // TOK_DEV)
    expert_ids_turns = jax.random.permutation(jax.random.fold_in(streams_of[2], 3), TOKENS // TOK_DEV)
    expert_ids = jax.vmap(lambda own, number: deal_out(jax.random.fold_in(streams_of[2], 2), own, number, TOK_DEV, EXPERTS, TOP, CAP, 2))(expert_ids_keys, expert_ids_turns).reshape((TOKENS, TOP))
    gates = jnp.clip(jnp.exp(math.log(0.5) - 2.3025851 * jax.random.uniform(streams_of[3], (TOKENS, TOP), jnp.float32) ** steps_of(streams_of[3], (TOKENS, TOP), ((0, 128),), -0.2, 0.2)), 0.05, 0.5)
    w_gate = noise(streams_of[4], (EXPERTS, D, H), D ** -0.5, 0.125, ((0, 64),))
    w_up = noise(streams_of[5], (EXPERTS, D, H), D ** -0.5, 0.125, ((0, 64),))
    w_down = noise(streams_of[6], (EXPERTS, H, D), H ** -0.5, 0.3125, ((0, 64),))
    return {"tokens": tokens, "cotangent": cotangent, "expert_ids": expert_ids, "gates": gates, "w_gate": w_gate, "w_up": w_up, "w_down": w_down}


def slot_table(expert_ids, n_experts, capacity):
    flat_ids = expert_ids.reshape(-1).astype(jnp.int32)
    assignments = flat_ids.shape[0]
    onehot = (flat_ids[:, None] == jnp.arange(n_experts, dtype=jnp.int32)[None, :]).astype(jnp.int32)
    before = jnp.cumsum(onehot, axis=0) - onehot
    slot_index = jnp.sum(before * onehot, axis=1).astype(jnp.int32)
    target = (flat_ids * capacity + slot_index).astype(jnp.int32)
    owners = jnp.full((n_experts * capacity,), -1, jnp.int32).at[target].set(jnp.arange(assignments, dtype=jnp.int32))
    return owners, target


def expert_forward(input_rows, w_gate_one, w_up_one, w_down_one):
    gate_pre = jnp.dot(input_rows, w_gate_one, preferred_element_type=jnp.float32)
    up_pre = jnp.dot(input_rows, w_up_one, preferred_element_type=jnp.float32)
    hidden = (jax.nn.silu(gate_pre) * up_pre).astype(jnp.bfloat16)
    expert_out = jnp.dot(hidden, w_down_one, preferred_element_type=jnp.float32).astype(jnp.bfloat16)
    return expert_out, gate_pre, up_pre, hidden


def hidden_grads(cot_rows, gate_pre, up_pre, w_down_one):
    hidden_grad = lax.dot_general(cot_rows, w_down_one, (((1,), (1,)), ((), ())), preferred_element_type=jnp.float32)
    sigmoid_gate = jax.nn.sigmoid(gate_pre)
    gate_grad = (hidden_grad * up_pre * sigmoid_gate * (1.0 + gate_pre * (1.0 - sigmoid_gate))).astype(jnp.bfloat16)
    up_grad = (hidden_grad * gate_pre * sigmoid_gate).astype(jnp.bfloat16)
    return gate_grad, up_grad


def row_grads(gate_grad, up_grad, w_gate_one, w_up_one):
    first = lax.dot_general(gate_grad, w_gate_one, (((1,), (1,)), ((), ())), preferred_element_type=jnp.float32)
    second = lax.dot_general(up_grad, w_up_one, (((1,), (1,)), ((), ())), preferred_element_type=jnp.float32)
    return (first + second).astype(jnp.bfloat16)


def reference(tokens, cotangent, expert_ids, gates, w_gate, w_up, w_down):
    devices = TOKENS // TOK_DEV
    per_dev = TOK_DEV * TOP
    owners, target = jax.vmap(partial(slot_table, n_experts=EXPERTS, capacity=CAP))(expert_ids.reshape(devices, TOK_DEV, TOP))
    owners = owners.reshape(devices, EXPERTS, CAP).transpose(1, 0, 2)
    offsets = (jnp.arange(devices, dtype=jnp.int32) * per_dev)[:, None]
    flat_gates = gates.reshape(-1)
    width = tokens.shape[1]

    def expert_step(totals, inputs):
        mixed_total, grad_total = totals
        owner_block, w_gate_one, w_up_one, w_down_one = inputs
        is_live = owner_block >= 0
        assign = jnp.where(is_live, owner_block + offsets, 0).reshape(-1).astype(jnp.int32)
        is_live = is_live.reshape(-1)
        token_index = (assign // TOP).astype(jnp.int32)
        input_rows = jnp.where(is_live[:, None], tokens[token_index], jnp.zeros((), tokens.dtype))
        weight = jnp.where(is_live, flat_gates[assign], jnp.zeros((), flat_gates.dtype))
        cot_rows = (weight[:, None] * cotangent[token_index].astype(jnp.float32)).astype(jnp.bfloat16)
        expert_out, gate_pre, up_pre, hidden = expert_forward(input_rows, w_gate_one, w_up_one, w_down_one)
        grad_down = jnp.dot(hidden.T, cot_rows, preferred_element_type=jnp.float32)
        gate_grad, up_grad = hidden_grads(cot_rows, gate_pre, up_pre, w_down_one)
        row_grad = row_grads(gate_grad, up_grad, w_gate_one, w_up_one)
        grad_gate = jnp.dot(input_rows.T, gate_grad, preferred_element_type=jnp.float32)
        grad_up = jnp.dot(input_rows.T, up_grad, preferred_element_type=jnp.float32)
        mixed_total = mixed_total.at[token_index].add(weight[:, None] * expert_out.astype(jnp.float32))
        grad_total = grad_total.at[token_index].add(row_grad.astype(jnp.float32))
        return (mixed_total, grad_total), (grad_gate, grad_up, grad_down)

    start = (jnp.zeros((TOKENS, width), jnp.float32), jnp.zeros((TOKENS, width), jnp.float32))
    totals, grads = lax.scan(expert_step, start, (owners, w_gate, w_up, w_down))
    mixed = totals[0].astype(jnp.bfloat16)
    input_grad = totals[1].astype(jnp.bfloat16)
    return (mixed, input_grad, grads[0], grads[1], grads[2])
```

```python
import jax
import jax.numpy as jnp
from jax import lax
from jax.experimental import pallas as pl
from jax.experimental.pallas import tpu as pltpu
from jax.sharding import Mesh, PartitionSpec as P

RING = 4
DEVS = 16
PAIRS = 8
CAP = 24
SLOTS = RING * 2 * CAP
VMEM = 44 << 20
F32, BF16 = jnp.float32, jnp.bfloat16


def shift(block, axis, by):
    return lax.ppermute(block, axis, [(i, (i + by) % RING) for i in range(RING)])


def near_gather(block, axis):
    return jnp.concatenate(
        [block, shift(block, axis, 1), shift(block, axis, -1), shift(block, axis, 2)], 0
    )


def ring_gather(block, axis):
    half = block.shape[0] // 2
    below, above = shift(block, axis, 1), shift(block, axis, -1)
    far_low, far_high = shift(below[:half], axis, 1), shift(above[half:], axis, -1)
    return jnp.concatenate([block, below, above, far_low, far_high], 0)


def ring_scatter(parts, axis):
    rows = parts.shape[0] // RING
    half = rows // 2
    own, below, above, far = (parts[i * rows : (i + 1) * rows] for i in range(RING))
    low = shift(far[:half], axis, 1).astype(F32)
    high = shift(far[half:], axis, -1).astype(F32)
    above = jnp.concatenate([(above[:half].astype(F32) + low).astype(BF16), above[half:]], 0)
    below = jnp.concatenate([below[:half], (below[half:].astype(F32) + high).astype(BF16)], 0)
    from_below = shift(above, axis, 1).astype(F32)
    from_above = shift(below, axis, -1).astype(F32)
    return (own.astype(F32) + from_below + from_above).astype(BF16)


def plane_gather(rows):
    width = rows.shape[1] // 2
    first = ring_gather(near_gather(rows[:, :width], "x"), "y")
    second = ring_gather(near_gather(rows[:, width:], "y"), "x")
    return first, second


def plane_scatter(first, second):
    first = ring_scatter(ring_scatter(first, "y"), "x")
    second = ring_scatter(ring_scatter(second, "x"), "y")
    return jnp.concatenate([first, second], 1)


def params():
    return pltpu.CompilerParams(vmem_limit_bytes=VMEM)


def cost(flops, nbytes):
    return pl.CostEstimate(flops=int(flops), bytes_accessed=int(nbytes), transcendentals=0)


def table_kernel(base_ref, table_ref, slot_ref, gate_ref):
    base = base_ref[0]
    row = lax.broadcasted_iota(jnp.int32, (256, 256), 0)
    col = lax.broadcasted_iota(jnp.int32, (256, 256), 1)
    before = jnp.where((row < col) & ((row < 128) == (col < 128)), 1.0, 0.0).astype(BF16)
    lane = lax.broadcasted_iota(jnp.int32, (RING, 256), 1)
    index = lax.broadcasted_iota(jnp.int32, (RING, 256), 0)
    for p in range(PAIRS):
        both = jnp.concatenate([table_ref[2 * p], table_ref[2 * p + 1]], 1)
        ids = both[:8].astype(jnp.int32)
        gates = both[8:]
        chosen, weight = [], []
        for j in range(RING):
            match = ids == base + j * DEVS
            chosen.append(jnp.sum(jnp.where(match, 1.0, 0.0), axis=0, keepdims=True))
            weight.append(jnp.sum(jnp.where(match, gates, 0.0), axis=0, keepdims=True))
        chosen = jnp.concatenate(chosen, 0)
        place = jnp.dot(chosen.astype(BF16), before, preferred_element_type=F32)
        slot = place.astype(jnp.int32) + jnp.where(lane < 128, 0, CAP) + index * (2 * CAP)
        slot_ref[p] = jnp.where(chosen > 0.5, slot, -1)
        gate_ref[p] = jnp.concatenate(weight, 0)


def slot_tables(base, table):
    shape = (PAIRS, RING, 256)
    return pl.pallas_call(
        table_kernel,
        out_shape=(jax.ShapeDtypeStruct(shape, jnp.int32), jax.ShapeDtypeStruct(shape, F32)),
        in_specs=[
            pl.BlockSpec(memory_space=pltpu.SMEM),
            pl.BlockSpec(memory_space=pltpu.VMEM),
        ],
        out_specs=(pl.BlockSpec(memory_space=pltpu.VMEM),) * 2,
        name="slot_tables",
        cost_estimate=cost(4e6, 1e6),
    )(base, table)


def spread(slot, values):
    row = lax.broadcasted_iota(jnp.int32, (SLOTS, 256), 0)
    total = jnp.zeros((SLOTS, 256), F32)
    for j in range(RING):
        value = 1.0 if values is None else values[j : j + 1, :]
        total = jnp.where(slot[j : j + 1, :] == row, value, total)
    return total


def take_kernel(weighted, slot_ref, gate_ref, first_ref, low_ref, high_ref, out_ref):
    slot = slot_ref[0]
    onehot = spread(slot, None).astype(BF16)
    width = first_ref.shape[1]
    left = jnp.dot(onehot, first_ref[...], preferred_element_type=F32)
    second = jnp.concatenate([low_ref[...], high_ref[...]], 0)
    right = jnp.dot(onehot, second, preferred_element_type=F32)
    if weighted:
        weight = jnp.sum(spread(slot, gate_ref[0]), axis=1, keepdims=True)
        left, right = left * weight, right * weight
    left, right = left.astype(BF16), right.astype(BF16)
    for j in range(RING):
        rows = slice(j * 2 * CAP, (j + 1) * 2 * CAP)
        out_ref[j, :, :width] = left[rows]
        out_ref[j, :, width:] = right[rows]


def pair_specs(width):
    table = pl.BlockSpec((1, RING, 256), lambda p: (p, 0, 0))
    return (
        table,
        pl.BlockSpec((256, width), lambda p: (p, 0)),
        pl.BlockSpec((128, width), lambda p: ((p % 2) * 8 + p // 2, 0)),
        pl.BlockSpec((128, width), lambda p: ((p % 2) * 8 + p // 2 + 4, 0)),
    )


def take_rows(slot, gate, first, second, weighted, name):
    width = first.shape[1]
    table, whole, low, high = pair_specs(width)
    return pl.pallas_call(
        lambda *refs: take_kernel(weighted, *refs),
        grid=(PAIRS,),
        out_shape=jax.ShapeDtypeStruct((RING, DEVS * CAP, 2 * width), BF16),
        in_specs=[table, table, whole, low, high],
        out_specs=pl.BlockSpec((RING, 2 * CAP, 2 * width), lambda p: (0, p, 0)),
        name=name,
        compiler_params=params(),
        cost_estimate=cost(3.2e9, 15e6),
    )(slot, gate, first, second, second)


def give_kernel(weighted, slot_ref, gate_ref, rows_ref, first_ref, second_ref):
    p = pl.program_id(0)
    slot = slot_ref[0]
    width = first_ref.shape[1]
    rows = rows_ref[...].reshape(SLOTS, 2 * width)
    dims = (((0,), (0,)), ((), ()))
    if weighted:
        weight = spread(slot, gate_ref[0])
        high = weight.astype(BF16)
        low = (weight - high.astype(F32)).astype(BF16)
        total = lax.dot_general(high, rows, dims, preferred_element_type=F32)
        total = total + lax.dot_general(low, rows, dims, preferred_element_type=F32)
    else:
        onehot = spread(slot, None).astype(BF16)
        total = lax.dot_general(onehot, rows, dims, preferred_element_type=F32)
    total = total.astype(BF16)
    first_ref[...] = total[:, :width]
    place = (p % 2) * 8 + p // 2
    second_ref[pl.ds(pl.multiple_of(place * 128, 128), 128), :] = total[:128, width:]
    second_ref[pl.ds(pl.multiple_of(place * 128 + 512, 128), 128), :] = total[128:, width:]


def give_rows(slot, gate, rows, weighted, name):
    width = rows.shape[2] // 2
    table, whole, _, _ = pair_specs(width)
    return pl.pallas_call(
        lambda *refs: give_kernel(weighted, *refs),
        grid=(PAIRS,),
        out_shape=(jax.ShapeDtypeStruct((DEVS * 128, width), BF16),) * 2,
        in_specs=[
            table,
            table,
            pl.BlockSpec((RING, 2 * CAP, 2 * width), lambda p: (0, p, 0)),
        ],
        out_specs=(whole, pl.BlockSpec((DEVS * 128, width), lambda p: (0, 0))),
        name=name,
        compiler_params=params(),
        cost_estimate=cost(3.2e9, 15e6),
    )(slot, gate, rows)


def per_expert(*shape):
    return pl.BlockSpec((1,) + shape, lambda e: (e,) + (0,) * len(shape))


def up_kernel(rows_ref, w_ref, hidden_ref, factor_ref):
    pre = jnp.dot(rows_ref[0], w_ref[0], preferred_element_type=F32)
    inner = pre.shape[1] // 2
    gate, up = pre[:, :inner], pre[:, inner:]
    sig = jax.nn.sigmoid(gate)
    silu = gate * sig
    hidden_ref[0] = (silu * up).astype(BF16)
    factor_ref[0, :, :inner] = up * sig * (1.0 + gate * (1.0 - sig))
    factor_ref[0, :, inner:] = silu


def up_project(rows, w_gu):
    count, cap, width = rows.shape
    two = w_gu.shape[2]
    return pl.pallas_call(
        up_kernel,
        grid=(count,),
        out_shape=(
            jax.ShapeDtypeStruct((count, cap, two // 2), BF16),
            jax.ShapeDtypeStruct((count, cap, two), F32),
        ),
        in_specs=[per_expert(cap, width), per_expert(width, two)],
        out_specs=(per_expert(cap, two // 2), per_expert(cap, two)),
        name="up_project",
        compiler_params=params(),
        cost_estimate=cost(8e9, 24e6),
    )(rows, w_gu)


def down_kernel(hidden_ref, w_ref, out_ref):
    out_ref[0] = jnp.dot(hidden_ref[0], w_ref[0], preferred_element_type=F32).astype(BF16)


def down_project(hidden, w_down):
    count, cap, inner = hidden.shape
    width = w_down.shape[2]
    return pl.pallas_call(
        down_kernel,
        grid=(count,),
        out_shape=jax.ShapeDtypeStruct((count, cap, width), BF16),
        in_specs=[per_expert(cap, inner), per_expert(inner, width)],
        out_specs=per_expert(cap, width),
        name="down_project",
        compiler_params=params(),
        cost_estimate=cost(4e9, 14e6),
    )(hidden, w_down)


def back_kernel(cot_ref, w_down_ref, factor_ref, w_gu_ref, grad_ref, row_ref):
    dims = (((1,), (1,)), ((), ()))
    hidden_grad = lax.dot_general(cot_ref[0], w_down_ref[0], dims, preferred_element_type=F32)
    inner = hidden_grad.shape[1]
    gate_grad = (hidden_grad * factor_ref[0, :, :inner]).astype(BF16)
    up_grad = (hidden_grad * factor_ref[0, :, inner:]).astype(BF16)
    both = jnp.concatenate([gate_grad, up_grad], 1)
    grad_ref[0] = both
    row = lax.dot_general(both, w_gu_ref[0], dims, preferred_element_type=F32)
    row_ref[0] = row.astype(BF16)


def back_project(cot_rows, w_down, factor, w_gu):
    count, cap, width = cot_rows.shape
    inner = w_down.shape[1]
    return pl.pallas_call(
        back_kernel,
        grid=(count,),
        out_shape=(
            jax.ShapeDtypeStruct((count, cap, 2 * inner), BF16),
            jax.ShapeDtypeStruct((count, cap, width), BF16),
        ),
        in_specs=[
            per_expert(cap, width),
            per_expert(inner, width),
            per_expert(cap, 2 * inner),
            per_expert(width, 2 * inner),
        ],
        out_specs=(per_expert(cap, 2 * inner), per_expert(cap, width)),
        name="back_project",
        compiler_params=params(),
        cost_estimate=cost(12e9, 40e6),
    )(cot_rows, w_down, factor, w_gu)


def outer_down_kernel(hidden_ref, cot_ref, out_ref):
    dims = (((0,), (0,)), ((), ()))
    total = lax.dot_general(hidden_ref[0], cot_ref[0], dims, preferred_element_type=F32)
    total = total.astype(BF16)
    half = total.shape[1] // 2
    out_ref[0, 0] = total[:, :half]
    out_ref[0, 1] = total[:, half:]


def outer_down(hidden, cot_rows):
    count, cap, inner = hidden.shape
    width = cot_rows.shape[2]
    return pl.pallas_call(
        outer_down_kernel,
        grid=(count,),
        out_shape=jax.ShapeDtypeStruct((count, 2, inner, width // 2), BF16),
        in_specs=[per_expert(cap, inner), per_expert(cap, width)],
        out_specs=per_expert(2, inner, width // 2),
        name="outer_down",
        compiler_params=params(),
        cost_estimate=cost(4e9, 14e6),
    )(hidden, cot_rows)


def outer_up_kernel(rows_ref, grad_ref, out_ref):
    dims = (((0,), (0,)), ((), ()))
    total = lax.dot_general(rows_ref[0], grad_ref[0], dims, preferred_element_type=F32)
    out_ref[0] = total.astype(BF16)


def outer_up(rows, grad):
    count, cap, width = rows.shape
    two = grad.shape[2]
    return pl.pallas_call(
        outer_up_kernel,
        grid=(count,),
        out_shape=jax.ShapeDtypeStruct((count, width, two), BF16),
        in_specs=[per_expert(cap, width), per_expert(cap, two)],
        out_specs=per_expert(width, two),
        name="outer_up",
        compiler_params=params(),
        cost_estimate=cost(8e9, 22e6),
    )(rows, grad)


def local(tokens, cotangent, expert_ids, gates, w_gate, w_up, w_down):
    width, inner = w_gate.shape[1:]
    core = lax.axis_index("edata")
    gate_half = lax.dynamic_slice_in_dim(w_gate[0], core * (width // 2), width // 2, 0)
    up_half = lax.dynamic_slice_in_dim(w_up[0], core * (width // 2), width // 2, 0)
    down_half = lax.dynamic_slice_in_dim(w_down[0], core * (inner // 2), inner // 2, 0)
    w_gu = lax.all_gather(
        jnp.concatenate([gate_half, up_half], 1), ("z", "edata"), axis=0, tiled=True
    ).reshape(RING, width, 2 * inner)
    w_dn = lax.all_gather(down_half, ("z", "edata"), axis=0, tiled=True).reshape(
        RING, inner, width
    )

    table = jnp.concatenate([expert_ids.T.astype(F32), gates.T], 0)
    table = near_gather(near_gather(table, "x"), "y").reshape(DEVS, 16, 128)
    base = lax.axis_index("y") * RING + lax.axis_index("x")
    slot, gate = slot_tables(base.reshape(1).astype(jnp.int32), table)

    tok_first, tok_second = plane_gather(tokens)
    cot_first, cot_second = plane_gather(cotangent)

    rows = take_rows(slot, gate, tok_first, tok_second, False, "take_tokens")
    hidden, factor = up_project(rows, w_gu)
    out_rows = down_project(hidden, w_dn)
    mixed = plane_scatter(*give_rows(slot, gate, out_rows, True, "give_out"))

    cot_rows = take_rows(slot, gate, cot_first, cot_second, True, "take_cot")
    grad, row_grad = back_project(cot_rows, w_dn, factor, w_gu)
    input_grad = plane_scatter(*give_rows(slot, gate, row_grad, False, "give_grad"))

    down = outer_down(hidden, cot_rows).reshape(2 * RING * inner, width // 2)
    down = lax.psum_scatter(down, ("z", "edata"), scatter_dimension=0, tiled=True)
    both = outer_up(rows, grad).reshape(RING * width, 2 * inner)
    both = lax.psum_scatter(both, ("z", "edata"), scatter_dimension=0, tiled=True)
    both = both.astype(F32)
    return (
        mixed,
        input_grad,
        both[None, :, :inner],
        both[None, :, inner:],
        down.astype(F32)[None],
    )


def solution(mesh):
    grid = Mesh(mesh.devices.reshape(RING, RING, RING, 2), ("z", "y", "x", "edata"))
    expert = ("z", "y", "x")
    rows = P(expert + ("edata",), None)
    weight = P(expert, None, None)
    return jax.shard_map(
        local,
        mesh=grid,
        in_specs=(rows, rows, rows, rows, weight, weight, weight),
        out_specs=(
            rows,
            rows,
            P(expert, "edata", None),
            P(expert, "edata", None),
            P(expert, None, "edata"),
        ),
        check_vma=False,
    )
```

```python
import jax
import jax.numpy as jnp
from jax import lax
from jax.experimental import pallas as pl
from jax.experimental.pallas import tpu as pltpu
from jax.sharding import Mesh, PartitionSpec as P

RING = 4
DEVS = 16
PAIRS = 8
CAP = 24
SLOTS = RING * 2 * CAP
BLOCK = 144
VMEM = 60 << 20
F32, BF16 = jnp.float32, jnp.bfloat16


def shift(block, axis, by):
    return lax.ppermute(block, axis, [(i, (i + by) % RING) for i in range(RING)])


def after(value, *others):
    return lax.optimization_barrier((value,) + others)[0]


def near(block, axis):
    return (block, shift(block, axis, 1), shift(block, axis, -1), shift(block, axis, 2))


def together(*groups):
    flat = lax.optimization_barrier(tuple(x for group in groups for x in group))
    out, at = [], 0
    for group in groups:
        out.append(flat[at : at + len(group)])
        at += len(group)
    return out


def sends(parts, axis):
    own, below, above, far = parts
    return (own, shift(above, axis, 1), shift(below, axis, -1), shift(far, axis, 2))


def total(parts):
    out = parts[0].astype(F32)
    for part in parts[1:]:
        out = out + part.astype(F32)
    return out.astype(BF16)


def cut(parts):
    rows = parts[0].shape[0] // RING
    return [total([part[i * rows : (i + 1) * rows] for part in parts]) for i in range(RING)]


def far_sends(parts, axis):
    return (shift(parts[3], axis, 1), shift(parts[4], axis, -1))


def side_sends(parts, pair, axis):
    own, below, above = parts[:3]
    half = pair[0].shape[0]
    above = jnp.concatenate([total((above[:half], pair[0])), above[half:]], 0)
    below = jnp.concatenate([below[:half], total((below[half:], pair[1]))], 0)
    return (own, shift(above, axis, 1), shift(below, axis, -1))


def params():
    return pltpu.CompilerParams(vmem_limit_bytes=VMEM)


def cost(flops, nbytes):
    return pl.CostEstimate(flops=int(flops), bytes_accessed=int(nbytes), transcendentals=0)


def piece(refs, outer, inner, rows):
    return refs[outer * 2 + inner // 2], (inner % 2) * rows


def make_tables(base, refs, slot_ref, gate_ref):
    row = lax.broadcasted_iota(jnp.int32, (256, 256), 0)
    col = lax.broadcasted_iota(jnp.int32, (256, 256), 1)
    before = jnp.where((row < col) & ((row < 128) == (col < 128)), 1.0, 0.0).astype(BF16)
    lane = lax.broadcasted_iota(jnp.int32, (RING, 256), 1)
    index = lax.broadcasted_iota(jnp.int32, (RING, 256), 0)
    for p in range(PAIRS):
        both = []
        for h in range(2):
            ref, first = piece(refs, p // 2, (p % 2) * 2 + h, BLOCK)
            both.append(ref[first + 128 : first + BLOCK, :256].astype(F32))
        ids = jnp.concatenate([t[:8, :128] for t in both], 1).astype(jnp.int32)
        gates = jnp.concatenate([t[8:, :128] + t[:8, 128:] + t[8:, 128:] for t in both], 1)
        chosen, weight = [], []
        for j in range(RING):
            match = ids == base + j * DEVS
            chosen.append(jnp.sum(jnp.where(match, 1.0, 0.0), axis=0, keepdims=True))
            weight.append(jnp.sum(jnp.where(match, gates, 0.0), axis=0, keepdims=True))
        chosen = jnp.concatenate(chosen, 0)
        place = jnp.dot(chosen.astype(BF16), before, preferred_element_type=F32)
        slot = place.astype(jnp.int32) + jnp.where(lane < 128, 0, CAP) + index * (2 * CAP)
        slot_ref[p] = jnp.where(chosen > 0.5, slot, -1)
        gate_ref[p] = jnp.concatenate(weight, 0)


def spread(slot, values):
    row = lax.broadcasted_iota(jnp.int32, (SLOTS, 256), 0)
    total = jnp.zeros((SLOTS, 256), F32)
    for j in range(RING):
        value = 1.0 if values is None else values[j : j + 1, :]
        total = jnp.where(slot[j : j + 1, :] == row, value, total)
    return total


def put_rows(out_ref, p, rows):
    for j in range(RING):
        out_ref[j, p * 2 * CAP : (p + 1) * 2 * CAP, :] = rows[j * 2 * CAP : (j + 1) * 2 * CAP]


def whole(*shape):
    return pl.BlockSpec(shape, lambda i: (0,) * len(shape))


def first_then(*shape):
    return pl.BlockSpec((1,) + shape, lambda i: (jnp.maximum(i - 1, 0),) + (0,) * len(shape))


def then_last(*shape):
    return pl.BlockSpec(
        (1,) + shape, lambda i: (jnp.minimum(i, RING - 1),) + (0,) * len(shape)
    )


def forward_kernel(base_ref, *refs):
    pieces, w_ref = refs[:8], refs[8]
    rows_ref, slot_ref, gate_ref, hidden_ref, factor_ref, held = refs[9:]
    step = pl.program_id(0)

    @pl.when(step == 0)
    def _():
        make_tables(base_ref[0], pieces, slot_ref, gate_ref)
        for p in range(PAIRS):
            onehot = spread(slot_ref[p], None).astype(BF16)
            blocks = []
            for h in range(2):
                ref, first = piece(pieces, p // 2, (p % 2) * 2 + h, BLOCK)
                blocks.append(ref[first : first + 128, :])
            tokens = jnp.concatenate(blocks, 0)
            put_rows(held, p, jnp.dot(onehot, tokens, preferred_element_type=F32).astype(BF16))

    @pl.when(step > 0)
    def _():
        rows = held[step - 1]
        rows_ref[0] = rows
        pre = jnp.dot(rows, w_ref[0], preferred_element_type=F32)
        inner = pre.shape[1] // 2
        gate, up = pre[:, :inner], pre[:, inner:]
        sig = jax.nn.sigmoid(gate)
        silu = gate * sig
        hidden_ref[0] = (silu * up).astype(BF16)
        factor_ref[0, :, :inner] = up * sig * (1.0 + gate * (1.0 - sig))
        factor_ref[0, :, inner:] = silu


def forward(base, pieces, w_gu):
    width, two = w_gu.shape[1:]
    cap = DEVS * CAP
    table = (PAIRS, RING, 256)
    return pl.pallas_call(
        forward_kernel,
        grid=(RING + 1,),
        out_shape=(
            jax.ShapeDtypeStruct((RING, cap, width), BF16),
            jax.ShapeDtypeStruct(table, jnp.int32),
            jax.ShapeDtypeStruct(table, F32),
            jax.ShapeDtypeStruct((RING, cap, two // 2), BF16),
            jax.ShapeDtypeStruct((RING, cap, two), F32),
        ),
        in_specs=[pl.BlockSpec(memory_space=pltpu.SMEM)]
        + [whole(*p.shape) for p in pieces]
        + [first_then(width, two)],
        out_specs=(
            first_then(cap, width),
            whole(*table),
            whole(*table),
            first_then(cap, two // 2),
            first_then(cap, two),
        ),
        scratch_shapes=[pltpu.VMEM((RING, cap, width), BF16)],
        name="forward",
        compiler_params=params(),
        cost_estimate=cost(11e9, 40e6),
    )(base, *pieces, w_gu)


def cot_kernel(slot_ref, gate_ref, *refs):
    pieces, hidden_ref, rows_ref, down_ref, held = refs[:8], *refs[8:]
    step = pl.program_id(0)

    @pl.when(step == 0)
    def _():
        for p in range(PAIRS):
            slot = slot_ref[p]
            onehot = spread(slot, None).astype(BF16)
            weight = jnp.sum(spread(slot, gate_ref[p]), axis=1, keepdims=True)
            blocks = []
            for h in range(2):
                ref, first = piece(pieces, (p % 2) * 2 + h, p // 2, 128)
                blocks.append(ref[first : first + 128, :])
            cot = jnp.concatenate(blocks, 0)
            rows = jnp.dot(onehot, cot, preferred_element_type=F32)
            put_rows(held, p, (rows * weight).astype(BF16))

    @pl.when(step > 0)
    def _():
        rows = held[step - 1]
        rows_ref[0] = rows
        dims = (((0,), (0,)), ((), ()))
        out = lax.dot_general(hidden_ref[0], rows, dims, preferred_element_type=F32)
        out = out.astype(BF16)
        half = out.shape[1] // 2
        down_ref[0, 0] = out[:, :half]
        down_ref[0, 1] = out[:, half:]


def take_cot(slot, gate, pieces, hidden):
    width = pieces[0].shape[1]
    cap, inner = hidden.shape[1:]
    table = (PAIRS, RING, 256)
    return pl.pallas_call(
        cot_kernel,
        grid=(RING + 1,),
        out_shape=(
            jax.ShapeDtypeStruct((RING, cap, width), BF16),
            jax.ShapeDtypeStruct((RING, 2, inner, width // 2), BF16),
        ),
        in_specs=[whole(*table)] * 2
        + [whole(*p.shape) for p in pieces]
        + [first_then(cap, inner)],
        out_specs=(first_then(cap, width), first_then(2, inner, width // 2)),
        scratch_shapes=[pltpu.VMEM((RING, cap, width), BF16)],
        name="take_cot",
        compiler_params=params(),
        cost_estimate=cost(6e9, 22e6),
    )(slot, gate, *pieces, hidden)


def part_of(refs, outer, inner):
    if outer < 3:
        return refs[outer], inner * 128
    return refs[3 + inner // 2], (inner % 2) * 128


def parts_of(width):
    big, small = (RING * 128, width), (RING * 64, width)
    return ((big,) * 3 + (small,) * 2) * 2


def give_rows(weighted, slot_ref, gate_ref, held, refs):
    width = held.shape[2] // 2
    dims = (((0,), (0,)), ((), ()))
    for p in range(PAIRS):
        slot = slot_ref[p]
        rows = held[:, p * 2 * CAP : (p + 1) * 2 * CAP, :].reshape(SLOTS, 2 * width)
        if weighted:
            weight = spread(slot, gate_ref[p])
            high = weight.astype(BF16)
            low = (weight - high.astype(F32)).astype(BF16)
            out = lax.dot_general(high, rows, dims, preferred_element_type=F32)
            out = out + lax.dot_general(low, rows, dims, preferred_element_type=F32)
        else:
            onehot = spread(slot, None).astype(BF16)
            out = lax.dot_general(onehot, rows, dims, preferred_element_type=F32)
        out = out.astype(BF16)
        for h in range(2):
            y, x = p // 2, (p % 2) * 2 + h
            block = out[h * 128 : (h + 1) * 128]
            ref, first = part_of(refs[:5], y, x)
            ref[first : first + 128, :] = block[:, :width]
            ref, first = part_of(refs[5:], x, y)
            ref[first : first + 128, :] = block[:, width:]


def out_kernel(slot_ref, gate_ref, hidden_ref, w_ref, *refs):
    step = pl.program_id(0)
    held = refs[10]

    @pl.when(step < RING)
    def _():
        out = jnp.dot(hidden_ref[0], w_ref[0], preferred_element_type=F32)
        held[step] = out.astype(BF16)

    @pl.when(step == RING)
    def _():
        give_rows(True, slot_ref, gate_ref, held, refs[:10])


def give_out(slot, gate, hidden, w_down):
    cap, inner = hidden.shape[1:]
    width = w_down.shape[2]
    table = (PAIRS, RING, 256)
    parts = parts_of(width // 2)
    return pl.pallas_call(
        out_kernel,
        grid=(RING + 1,),
        out_shape=tuple(jax.ShapeDtypeStruct(part, BF16) for part in parts),
        in_specs=[whole(*table)] * 2 + [then_last(cap, inner), then_last(inner, width)],
        out_specs=tuple(whole(*part) for part in parts),
        scratch_shapes=[pltpu.VMEM((RING, cap, width), BF16)],
        name="give_out",
        compiler_params=params(),
        cost_estimate=cost(9e9, 20e6),
    )(slot, gate, hidden, w_down)


def back_kernel(slot_ref, gate_ref, cot_ref, w_down_ref, factor_ref, w_gu_ref, *refs):
    step = pl.program_id(0)
    grad_ref, held = refs[10], refs[11]
    dims = (((1,), (1,)), ((), ()))

    @pl.when(step < RING)
    def _():
        hidden_grad = lax.dot_general(
            cot_ref[0], w_down_ref[0], dims, preferred_element_type=F32
        )
        inner = hidden_grad.shape[1]
        gate_grad = (hidden_grad * factor_ref[0, :, :inner]).astype(BF16)
        up_grad = (hidden_grad * factor_ref[0, :, inner:]).astype(BF16)
        both = jnp.concatenate([gate_grad, up_grad], 1)
        grad_ref[0] = both
        row = lax.dot_general(both, w_gu_ref[0], dims, preferred_element_type=F32)
        held[step] = row.astype(BF16)

    @pl.when(step == RING)
    def _():
        give_rows(False, slot_ref, gate_ref, held, refs[:10])


def give_back(slot, gate, cot_rows, w_down, factor, w_gu):
    cap, width = cot_rows.shape[1:]
    inner = w_down.shape[1]
    table = (PAIRS, RING, 256)
    parts = parts_of(width // 2)
    out = pl.pallas_call(
        back_kernel,
        grid=(RING + 1,),
        out_shape=tuple(jax.ShapeDtypeStruct(part, BF16) for part in parts)
        + (jax.ShapeDtypeStruct((RING, cap, 2 * inner), BF16),),
        in_specs=[whole(*table)] * 2
        + [
            then_last(cap, width),
            then_last(inner, width),
            then_last(cap, 2 * inner),
            then_last(width, 2 * inner),
        ],
        out_specs=tuple(whole(*part) for part in parts) + (then_last(cap, 2 * inner),),
        scratch_shapes=[pltpu.VMEM((RING, cap, width), BF16)],
        name="give_back",
        compiler_params=params(),
        cost_estimate=cost(15e9, 45e6),
    )(slot, gate, cot_rows, w_down, factor, w_gu)
    return out[:10], out[10]


def per_expert(*shape):
    return pl.BlockSpec((1,) + shape, lambda e: (e,) + (0,) * len(shape))


def outer_up_kernel(rows_ref, grad_ref, out_ref):
    dims = (((0,), (0,)), ((), ()))
    total = lax.dot_general(rows_ref[0], grad_ref[0], dims, preferred_element_type=F32)
    out_ref[0] = total.astype(BF16)


def outer_up(rows, grad):
    count, cap, width = rows.shape
    two = grad.shape[2]
    return pl.pallas_call(
        outer_up_kernel,
        grid=(count,),
        out_shape=jax.ShapeDtypeStruct((count, width, two), BF16),
        in_specs=[per_expert(cap, width), per_expert(cap, two)],
        out_specs=per_expert(width, two),
        name="outer_up",
        compiler_params=params(),
        cost_estimate=cost(8e9, 22e6),
    )(rows, grad)


def local(tokens, cotangent, expert_ids, gates, w_gate, w_up, w_down):
    width, inner = w_gate.shape[1:]
    half = width // 2
    core = lax.axis_index("edata")
    gate_half = lax.dynamic_slice_in_dim(w_gate[0], core * half, half, 0)
    up_half = lax.dynamic_slice_in_dim(w_up[0], core * half, half, 0)
    down_half = lax.dynamic_slice_in_dim(w_down[0], core * (inner // 2), inner // 2, 0)
    w_gu = lax.all_gather(
        jnp.concatenate([gate_half, up_half], 1), ("z", "edata"), axis=0, tiled=True
    ).reshape(RING, width, 2 * inner)
    w_dn = lax.all_gather(down_half, ("z", "edata"), axis=0, tiled=True).reshape(
        RING, inner, width
    )

    hi = lax.reduce_precision(gates.T, 8, 7)
    mid = lax.reduce_precision(gates.T - hi, 8, 7)
    ids = expert_ids.T.astype(F32)
    left = jnp.concatenate([ids, hi], 0)
    right = jnp.concatenate([mid, gates.T - hi - mid], 0)
    table = jnp.concatenate([left, right], 1).astype(BF16)
    table = jnp.pad(table, ((0, 0), (0, width - table.shape[1])))
    own_t, own_c = jnp.concatenate([tokens, table], 0), cotangent
    below_t, below_c = shift(own_t, "x", 1), shift(own_c, "y", 1)
    above_t, above_c = shift(own_t, "x", -1), shift(own_c, "y", -1)
    (own_t, below_t, above_t), (own_c, below_c, above_c) = together(
        (own_t, below_t, above_t), (own_c, below_c, above_c)
    )
    low_t, low_c = jnp.concatenate([own_t, below_t], 0), jnp.concatenate([own_c, below_c], 0)
    first_t = (shift(low_t, "y", 1), shift(low_t, "y", -1))
    first_c = (shift(low_c, "x", 1), shift(low_c, "x", -1))
    over_t = shift(own_t, "x", 2)
    over_c = shift(after(own_c, over_t), "y", 2)
    first_t, first_c, (above_t, above_c, over_t, over_c) = together(
        first_t, first_c, (above_t, above_c, over_t, over_c)
    )
    high_t, high_c = jnp.concatenate([above_t, over_t], 0), jnp.concatenate([above_c, over_c], 0)
    second_t = (shift(high_t, "y", 1), shift(high_t, "y", -1))
    second_c = (shift(high_c, "x", 1), shift(high_c, "x", -1))
    third_t, third_c = shift(first_t[0], "y", 1), shift(first_c[0], "x", 1)
    fourth_t, fourth_c = shift(second_t[1], "y", -1), shift(second_c[1], "x", -1)
    tok = (low_t, high_t, first_t[0], second_t[0], first_t[1], second_t[1], third_t, fourth_t)
    cot = (low_c, high_c, first_c[0], second_c[0], first_c[1], second_c[1], third_c, fourth_c)

    base = lax.axis_index("y") * RING + lax.axis_index("x")
    rows, slot, gate, hidden, factor = forward(base.reshape(1).astype(jnp.int32), tok, w_gu)
    out = give_out(slot, gate, hidden, w_dn)
    out_1, out_2 = out[:5], out[5:]
    far_1, far_2 = far_sends(out_1, "y"), far_sends(out_2, "x")
    cot_rows, down = take_cot(after(slot, *out), gate, cot, hidden)
    far_1, far_2, (cot_rows, down) = together(far_1, far_2, (cot_rows, down))
    down = down.reshape(2 * RING * inner, half)
    down_sum = lax.psum_scatter(down, ("z", "edata"), scatter_dimension=0, tiled=True)

    side_1, side_2 = side_sends(out_1, far_1, "y"), side_sends(out_2, far_2, "x")
    gin, grad = give_back(slot, gate, cot_rows, w_dn, factor, w_gu)
    side_1, side_2, gin, (grad,) = together(side_1, side_2, gin, (grad,))

    gin_1, gin_2 = gin[:5], gin[5:]
    far_1, far_2 = far_sends(gin_1, "y"), far_sends(gin_2, "x")
    near_1, near_2 = sends(cut(side_1), "x"), sends(cut(side_2), "y")
    both = outer_up(rows, grad).reshape(RING * width, 2 * inner)
    both_sum = lax.psum_scatter(both, ("z", "edata"), scatter_dimension=0, tiled=True)
    near_1, near_2, far_1, far_2 = together(near_1, near_2, far_1, far_2)

    side_1, side_2 = side_sends(gin_1, far_1, "y"), side_sends(gin_2, far_2, "x")
    last_1, last_2 = sends(cut(side_1), "x"), sends(cut(side_2), "y")
    mixed = jnp.concatenate([total(near_1), total(near_2)], 1)
    input_grad = jnp.concatenate([total(last_1), total(last_2)], 1)

    both_sum = both_sum.astype(F32)
    return (
        mixed,
        input_grad,
        both_sum[None, :, :inner],
        both_sum[None, :, inner:],
        down_sum.astype(F32)[None],
    )


def solution(mesh):
    grid = Mesh(mesh.devices.reshape(RING, RING, RING, 2), ("z", "y", "x", "edata"))
    expert = ("z", "y", "x")
    rows = P(expert + ("edata",), None)
    weight = P(expert, None, None)
    return jax.shard_map(
        local,
        mesh=grid,
        in_specs=(rows, rows, rows, rows, weight, weight, weight),
        out_specs=(
            rows,
            rows,
            P(expert, "edata", None),
            P(expert, "edata", None),
            P(expert, None, "edata"),
        ),
        check_vma=False,
    )
```

```python
import jax
import jax.numpy as jnp
from jax import lax
from jax.experimental import pallas as pl
from jax.experimental.pallas import tpu as pltpu
from jax.sharding import Mesh, PartitionSpec as P

RING = 4
DEVS = 16
PAIRS = 8
CAP = 24
SLOTS = RING * 2 * CAP
BLOCK = 144
VMEM = 60 << 20
F32, BF16 = jnp.float32, jnp.bfloat16


def shift(block, axis, by):
    return lax.ppermute(block, axis, [(i, (i + by) % RING) for i in range(RING)])


def after(value, *others):
    return lax.optimization_barrier((value,) + others)[0]


def near(block, axis):
    return (block, shift(block, axis, 1), shift(block, axis, -1), shift(block, axis, 2))


def together(*groups):
    flat = lax.optimization_barrier(tuple(x for group in groups for x in group))
    out, at = [], 0
    for group in groups:
        out.append(flat[at : at + len(group)])
        at += len(group)
    return out


def sides(whole, axis):
    return (shift(whole, axis, 1), shift(whole, axis, -1))


def fars(pair, axis):
    half = pair[0].shape[0] // 2
    return (shift(pair[0][:half], axis, 1), shift(pair[1][half:], axis, -1))


def sends(parts, axis):
    own, below, above, far = parts
    return (own, shift(above, axis, 1), shift(below, axis, -1), shift(far, axis, 2))


def total(parts):
    out = parts[0].astype(F32)
    for part in parts[1:]:
        out = out + part.astype(F32)
    return out.astype(BF16)


def cut(parts):
    rows = parts[0].shape[0] // RING
    return [total([part[i * rows : (i + 1) * rows] for part in parts]) for i in range(RING)]


def far_sends(parts, axis):
    return (shift(parts[3], axis, 1), shift(parts[4], axis, -1))


def side_sends(parts, pair, axis):
    own, below, above = parts[:3]
    half = pair[0].shape[0]
    above = jnp.concatenate([total((above[:half], pair[0])), above[half:]], 0)
    below = jnp.concatenate([below[:half], total((below[half:], pair[1]))], 0)
    return (own, shift(above, axis, 1), shift(below, axis, -1))


def params():
    return pltpu.CompilerParams(vmem_limit_bytes=VMEM)


def cost(flops, nbytes):
    return pl.CostEstimate(flops=int(flops), bytes_accessed=int(nbytes), transcendentals=0)


def piece(refs, outer, inner, rows):
    if outer < 3:
        return refs[outer], inner * rows
    return refs[3 + inner // 2], (inner % 2) * rows


def pair_blocks(refs, p, rows):
    left, right = [], []
    for h in range(2):
        y, x = p // 2, (p % 2) * 2 + h
        ref, first = piece(refs[:5], y, x, rows)
        left.append(ref[first : first + 128, :])
        ref, first = piece(refs[5:], x, y, 128)
        right.append(ref[first : first + 128, :])
    return jnp.concatenate(left, 0), jnp.concatenate(right, 0)


def make_tables(base, refs, slot_ref, gate_ref):
    row = lax.broadcasted_iota(jnp.int32, (256, 256), 0)
    col = lax.broadcasted_iota(jnp.int32, (256, 256), 1)
    before = jnp.where((row < col) & ((row < 128) == (col < 128)), 1.0, 0.0).astype(BF16)
    lane = lax.broadcasted_iota(jnp.int32, (RING, 256), 1)
    index = lax.broadcasted_iota(jnp.int32, (RING, 256), 0)
    for p in range(PAIRS):
        both = []
        for h in range(2):
            ref, first = piece(refs[:5], p // 2, (p % 2) * 2 + h, BLOCK)
            both.append(ref[first + 128 : first + BLOCK, :256].astype(F32))
        ids = jnp.concatenate([t[:8, :128] for t in both], 1).astype(jnp.int32)
        gates = jnp.concatenate([t[8:, :128] + t[:8, 128:] + t[8:, 128:] for t in both], 1)
        chosen, weight = [], []
        for j in range(RING):
            match = ids == base + j * DEVS
            chosen.append(jnp.sum(jnp.where(match, 1.0, 0.0), axis=0, keepdims=True))
            weight.append(jnp.sum(jnp.where(match, gates, 0.0), axis=0, keepdims=True))
        chosen = jnp.concatenate(chosen, 0)
        place = jnp.dot(chosen.astype(BF16), before, preferred_element_type=F32)
        slot = place.astype(jnp.int32) + jnp.where(lane < 128, 0, CAP) + index * (2 * CAP)
        slot_ref[p] = jnp.where(chosen > 0.5, slot, -1)
        gate_ref[p] = jnp.concatenate(weight, 0)


def spread(slot, values):
    row = lax.broadcasted_iota(jnp.int32, (SLOTS, 256), 0)
    total = jnp.zeros((SLOTS, 256), F32)
    for j in range(RING):
        value = 1.0 if values is None else values[j : j + 1, :]
        total = jnp.where(slot[j : j + 1, :] == row, value, total)
    return total


def put_rows(out_ref, p, left, right):
    width = left.shape[1]
    for j in range(RING):
        rows = slice(p * 2 * CAP, (p + 1) * 2 * CAP)
        part = slice(j * 2 * CAP, (j + 1) * 2 * CAP)
        out_ref[j, rows, :width] = left[part]
        out_ref[j, rows, width:] = right[part]


def whole(*shape):
    return pl.BlockSpec(shape, lambda i: (0,) * len(shape))


def first_then(*shape):
    return pl.BlockSpec((1,) + shape, lambda i: (jnp.maximum(i - 1, 0),) + (0,) * len(shape))


def then_last(*shape):
    return pl.BlockSpec(
        (1,) + shape, lambda i: (jnp.minimum(i, RING - 1),) + (0,) * len(shape)
    )


def forward_kernel(base_ref, *refs):
    pieces, w_ref = refs[:10], refs[10]
    rows_ref, slot_ref, gate_ref, hidden_ref, factor_ref, held = refs[11:]
    step = pl.program_id(0)

    @pl.when(step == 0)
    def _():
        make_tables(base_ref[0], pieces, slot_ref, gate_ref)
        for p in range(PAIRS):
            onehot = spread(slot_ref[p], None).astype(BF16)
            left, right = (
                jnp.dot(onehot, block, preferred_element_type=F32).astype(BF16)
                for block in pair_blocks(pieces, p, BLOCK)
            )
            put_rows(held, p, left, right)

    @pl.when(step > 0)
    def _():
        rows = held[step - 1]
        rows_ref[0] = rows
        pre = jnp.dot(rows, w_ref[0], preferred_element_type=F32)
        inner = pre.shape[1] // 2
        gate, up = pre[:, :inner], pre[:, inner:]
        sig = jax.nn.sigmoid(gate)
        silu = gate * sig
        hidden_ref[0] = (silu * up).astype(BF16)
        factor_ref[0, :, :inner] = up * sig * (1.0 + gate * (1.0 - sig))
        factor_ref[0, :, inner:] = silu


def forward(base, pieces, w_gu):
    width, two = w_gu.shape[1:]
    cap = DEVS * CAP
    table = (PAIRS, RING, 256)
    return pl.pallas_call(
        forward_kernel,
        grid=(RING + 1,),
        out_shape=(
            jax.ShapeDtypeStruct((RING, cap, width), BF16),
            jax.ShapeDtypeStruct(table, jnp.int32),
            jax.ShapeDtypeStruct(table, F32),
            jax.ShapeDtypeStruct((RING, cap, two // 2), BF16),
            jax.ShapeDtypeStruct((RING, cap, two), F32),
        ),
        in_specs=[pl.BlockSpec(memory_space=pltpu.SMEM)]
        + [whole(*p.shape) for p in pieces]
        + [first_then(width, two)],
        out_specs=(
            first_then(cap, width),
            whole(*table),
            whole(*table),
            first_then(cap, two // 2),
            first_then(cap, two),
        ),
        scratch_shapes=[pltpu.VMEM((RING, cap, width), BF16)],
        name="forward",
        compiler_params=params(),
        cost_estimate=cost(11e9, 40e6),
    )(base, *pieces, w_gu)


def cot_kernel(slot_ref, gate_ref, *refs):
    pieces, hidden_ref, rows_ref, down_ref, held = refs[:10], *refs[10:]
    step = pl.program_id(0)

    @pl.when(step == 0)
    def _():
        for p in range(PAIRS):
            slot = slot_ref[p]
            onehot = spread(slot, None).astype(BF16)
            weight = jnp.sum(spread(slot, gate_ref[p]), axis=1, keepdims=True)
            left, right = (
                (jnp.dot(onehot, block, preferred_element_type=F32) * weight).astype(BF16)
                for block in pair_blocks(pieces, p, 128)
            )
            put_rows(held, p, left, right)

    @pl.when(step > 0)
    def _():
        rows = held[step - 1]
        rows_ref[0] = rows
        dims = (((0,), (0,)), ((), ()))
        out = lax.dot_general(hidden_ref[0], rows, dims, preferred_element_type=F32)
        out = out.astype(BF16)
        half = out.shape[1] // 2
        down_ref[0, 0] = out[:, :half]
        down_ref[0, 1] = out[:, half:]


def take_cot(slot, gate, pieces, hidden):
    width = 2 * pieces[0].shape[1]
    cap, inner = hidden.shape[1:]
    table = (PAIRS, RING, 256)
    return pl.pallas_call(
        cot_kernel,
        grid=(RING + 1,),
        out_shape=(
            jax.ShapeDtypeStruct((RING, cap, width), BF16),
            jax.ShapeDtypeStruct((RING, 2, inner, width // 2), BF16),
        ),
        in_specs=[whole(*table)] * 2
        + [whole(*p.shape) for p in pieces]
        + [first_then(cap, inner)],
        out_specs=(first_then(cap, width), first_then(2, inner, width // 2)),
        scratch_shapes=[pltpu.VMEM((RING, cap, width), BF16)],
        name="take_cot",
        compiler_params=params(),
        cost_estimate=cost(6e9, 22e6),
    )(slot, gate, *pieces, hidden)


def parts_of(width):
    big, small = (RING * 128, width), (RING * 64, width)
    return ((big,) * 3 + (small,) * 2) * 2


def give_rows(weighted, slot_ref, gate_ref, held, refs):
    width = held.shape[2] // 2
    dims = (((0,), (0,)), ((), ()))
    for p in range(PAIRS):
        slot = slot_ref[p]
        rows = held[:, p * 2 * CAP : (p + 1) * 2 * CAP, :].reshape(SLOTS, 2 * width)
        if weighted:
            weight = spread(slot, gate_ref[p])
            high = weight.astype(BF16)
            low = (weight - high.astype(F32)).astype(BF16)
            out = lax.dot_general(high, rows, dims, preferred_element_type=F32)
            out = out + lax.dot_general(low, rows, dims, preferred_element_type=F32)
        else:
            onehot = spread(slot, None).astype(BF16)
            out = lax.dot_general(onehot, rows, dims, preferred_element_type=F32)
        out = out.astype(BF16)
        for h in range(2):
            y, x = p // 2, (p % 2) * 2 + h
            block = out[h * 128 : (h + 1) * 128]
            ref, first = piece(refs[:5], y, x, 128)
            ref[first : first + 128, :] = block[:, :width]
            ref, first = piece(refs[5:], x, y, 128)
            ref[first : first + 128, :] = block[:, width:]


def out_kernel(slot_ref, gate_ref, hidden_ref, w_ref, *refs):
    step = pl.program_id(0)
    held = refs[10]

    @pl.when(step < RING)
    def _():
        out = jnp.dot(hidden_ref[0], w_ref[0], preferred_element_type=F32)
        held[step] = out.astype(BF16)

    @pl.when(step == RING)
    def _():
        give_rows(True, slot_ref, gate_ref, held, refs[:10])


def give_out(slot, gate, hidden, w_down):
    cap, inner = hidden.shape[1:]
    width = w_down.shape[2]
    table = (PAIRS, RING, 256)
    parts = parts_of(width // 2)
    return pl.pallas_call(
        out_kernel,
        grid=(RING + 1,),
        out_shape=tuple(jax.ShapeDtypeStruct(part, BF16) for part in parts),
        in_specs=[whole(*table)] * 2 + [then_last(cap, inner), then_last(inner, width)],
        out_specs=tuple(whole(*part) for part in parts),
        scratch_shapes=[pltpu.VMEM((RING, cap, width), BF16)],
        name="give_out",
        compiler_params=params(),
        cost_estimate=cost(9e9, 20e6),
    )(slot, gate, hidden, w_down)


def back_kernel(slot_ref, gate_ref, cot_ref, w_down_ref, factor_ref, w_gu_ref, *refs):
    step = pl.program_id(0)
    grad_ref, held = refs[10], refs[11]
    dims = (((1,), (1,)), ((), ()))

    @pl.when(step < RING)
    def _():
        hidden_grad = lax.dot_general(
            cot_ref[0], w_down_ref[0], dims, preferred_element_type=F32
        )
        inner = hidden_grad.shape[1]
        gate_grad = (hidden_grad * factor_ref[0, :, :inner]).astype(BF16)
        up_grad = (hidden_grad * factor_ref[0, :, inner:]).astype(BF16)
        both = jnp.concatenate([gate_grad, up_grad], 1)
        grad_ref[0] = both
        row = lax.dot_general(both, w_gu_ref[0], dims, preferred_element_type=F32)
        held[step] = row.astype(BF16)

    @pl.when(step == RING)
    def _():
        give_rows(False, slot_ref, gate_ref, held, refs[:10])


def give_back(slot, gate, cot_rows, w_down, factor, w_gu):
    cap, width = cot_rows.shape[1:]
    inner = w_down.shape[1]
    table = (PAIRS, RING, 256)
    parts = parts_of(width // 2)
    out = pl.pallas_call(
        back_kernel,
        grid=(RING + 1,),
        out_shape=tuple(jax.ShapeDtypeStruct(part, BF16) for part in parts)
        + (jax.ShapeDtypeStruct((RING, cap, 2 * inner), BF16),),
        in_specs=[whole(*table)] * 2
        + [
            then_last(cap, width),
            then_last(inner, width),
            then_last(cap, 2 * inner),
            then_last(width, 2 * inner),
        ],
        out_specs=tuple(whole(*part) for part in parts) + (then_last(cap, 2 * inner),),
        scratch_shapes=[pltpu.VMEM((RING, cap, width), BF16)],
        name="give_back",
        compiler_params=params(),
        cost_estimate=cost(15e9, 45e6),
    )(slot, gate, cot_rows, w_down, factor, w_gu)
    return out[:10], out[10]


def per_expert(*shape):
    return pl.BlockSpec((1,) + shape, lambda e: (e,) + (0,) * len(shape))


def outer_up_kernel(rows_ref, grad_ref, out_ref):
    dims = (((0,), (0,)), ((), ()))
    total = lax.dot_general(rows_ref[0], grad_ref[0], dims, preferred_element_type=F32)
    out_ref[0] = total.astype(BF16)


def outer_up(rows, grad):
    count, cap, width = rows.shape
    two = grad.shape[2]
    return pl.pallas_call(
        outer_up_kernel,
        grid=(count,),
        out_shape=jax.ShapeDtypeStruct((count, width, two), BF16),
        in_specs=[per_expert(cap, width), per_expert(cap, two)],
        out_specs=per_expert(width, two),
        name="outer_up",
        compiler_params=params(),
        cost_estimate=cost(8e9, 22e6),
    )(rows, grad)


def local(tokens, cotangent, expert_ids, gates, w_gate, w_up, w_down):
    width, inner = w_gate.shape[1:]
    half = width // 2
    core = lax.axis_index("edata")
    gate_half = lax.dynamic_slice_in_dim(w_gate[0], core * half, half, 0)
    up_half = lax.dynamic_slice_in_dim(w_up[0], core * half, half, 0)
    down_half = lax.dynamic_slice_in_dim(w_down[0], core * (inner // 2), inner // 2, 0)
    w_gu = lax.all_gather(
        jnp.concatenate([gate_half, up_half], 1), ("z", "edata"), axis=0, tiled=True
    ).reshape(RING, width, 2 * inner)
    w_dn = lax.all_gather(down_half, ("z", "edata"), axis=0, tiled=True).reshape(
        RING, inner, width
    )

    hi = lax.reduce_precision(gates.T, 8, 7)
    mid = lax.reduce_precision(gates.T - hi, 8, 7)
    ids = expert_ids.T.astype(F32)
    left = jnp.concatenate([ids, hi], 0)
    right = jnp.concatenate([mid, gates.T - hi - mid], 0)
    table = jnp.concatenate([left, right], 1).astype(BF16)
    table = jnp.pad(table, ((0, 0), (0, half - table.shape[1])))
    near_1 = near(jnp.concatenate([tokens[:, :half], table, cotangent[:, :half]], 0), "x")
    near_2 = near(jnp.concatenate([tokens[:, half:], cotangent[:, half:]], 0), "y")
    near_1, near_2 = together(near_1, near_2)
    tok_1 = jnp.concatenate([block[:BLOCK] for block in near_1], 0)
    tok_2 = jnp.concatenate([block[:128] for block in near_2], 0)
    cot_1 = jnp.concatenate([block[BLOCK:] for block in near_1], 0)
    cot_2 = jnp.concatenate([block[128:] for block in near_2], 0)

    side_1, side_2 = sides(tok_1, "y"), sides(tok_2, "x")
    side_1, side_2, (cot_1, cot_2) = together(side_1, side_2, (cot_1, cot_2))
    far_1, far_2 = fars(side_1, "y"), fars(side_2, "x")
    tok = (tok_1,) + side_1 + far_1 + (tok_2,) + side_2 + far_2

    base = lax.axis_index("y") * RING + lax.axis_index("x")
    rows, slot, gate, hidden, factor = forward(base.reshape(1).astype(jnp.int32), tok, w_gu)
    side_1, side_2 = sides(cot_1, "y"), sides(cot_2, "x")
    side_1, side_2, (rows, slot, gate, hidden, factor) = together(
        side_1, side_2, (rows, slot, gate, hidden, factor)
    )
    far_1, far_2 = fars(side_1, "y"), fars(side_2, "x")
    cot = (cot_1,) + side_1 + far_1 + (cot_2,) + side_2 + far_2

    out = give_out(slot, gate, hidden, w_dn)
    out_1, out_2 = out[:5], out[5:]
    far_1, far_2 = far_sends(out_1, "y"), far_sends(out_2, "x")
    cot_rows, down = take_cot(after(slot, *out), gate, cot, hidden)
    far_1, far_2, (cot_rows, down) = together(far_1, far_2, (cot_rows, down))
    down = down.reshape(2 * RING * inner, half)
    down_sum = lax.psum_scatter(down, ("z", "edata"), scatter_dimension=0, tiled=True)

    side_1, side_2 = side_sends(out_1, far_1, "y"), side_sends(out_2, far_2, "x")
    gin, grad = give_back(slot, gate, cot_rows, w_dn, factor, w_gu)
    side_1, side_2, gin, (grad,) = together(side_1, side_2, gin, (grad,))

    gin_1, gin_2 = gin[:5], gin[5:]
    far_1, far_2 = far_sends(gin_1, "y"), far_sends(gin_2, "x")
    near_1, near_2 = sends(cut(side_1), "x"), sends(cut(side_2), "y")
    both = outer_up(rows, grad).reshape(RING * width, 2 * inner)
    both_sum = lax.psum_scatter(both, ("z", "edata"), scatter_dimension=0, tiled=True)
    near_1, near_2, far_1, far_2 = together(near_1, near_2, far_1, far_2)

    side_1, side_2 = side_sends(gin_1, far_1, "y"), side_sends(gin_2, far_2, "x")
    last_1, last_2 = sends(cut(side_1), "x"), sends(cut(side_2), "y")
    mixed = jnp.concatenate([total(near_1), total(near_2)], 1)
    input_grad = jnp.concatenate([total(last_1), total(last_2)], 1)

    both_sum = both_sum.astype(F32)
    return (
        mixed,
        input_grad,
        both_sum[None, :, :inner],
        both_sum[None, :, inner:],
        down_sum.astype(F32)[None],
    )


def solution(mesh):
    grid = Mesh(mesh.devices.reshape(RING, RING, RING, 2), ("z", "y", "x", "edata"))
    expert = ("z", "y", "x")
    rows = P(expert + ("edata",), None)
    weight = P(expert, None, None)
    return jax.shard_map(
        local,
        mesh=grid,
        in_specs=(rows, rows, rows, rows, weight, weight, weight),
        out_specs=(
            rows,
            rows,
            P(expert, "edata", None),
            P(expert, "edata", None),
            P(expert, None, "edata"),
        ),
        check_vma=False,
    )
```

```python
import jax
import jax.numpy as jnp
from jax import lax
from jax.experimental import pallas as pl
from jax.experimental.pallas import tpu as pltpu
from jax.sharding import Mesh, PartitionSpec as P

RING = 4
DEVS = 16
PAIRS = 8
CAP = 24
SLOTS = RING * 2 * CAP
BLOCK = 144
VMEM = 42 << 20
F32, BF16 = jnp.float32, jnp.bfloat16


def shift(block, axis, by):
    return lax.ppermute(block, axis, [(i, (i + by) % RING) for i in range(RING)])


def after(value, *others):
    return lax.optimization_barrier((value,) + others)[0]


def near(block, axis):
    return (block, shift(block, axis, 1), shift(block, axis, -1), shift(block, axis, 2))


def together(*groups):
    flat = lax.optimization_barrier(tuple(x for group in groups for x in group))
    out, at = [], 0
    for group in groups:
        out.append(flat[at : at + len(group)])
        at += len(group)
    return out


def sides(whole, axis):
    return (shift(whole, axis, 1), shift(whole, axis, -1))


def fars(pair, axis):
    half = pair[0].shape[0] // 2
    return (shift(pair[0][:half], axis, 1), shift(pair[1][half:], axis, -1))


def sends(parts, axis):
    own, below, above, far = parts
    return (own, shift(above, axis, 1), shift(below, axis, -1), shift(far, axis, 2))


def total(parts):
    out = parts[0].astype(F32)
    for part in parts[1:]:
        out = out + part.astype(F32)
    return out.astype(BF16)


def cut(parts):
    rows = parts[0].shape[0] // RING
    return [total([part[i * rows : (i + 1) * rows] for part in parts]) for i in range(RING)]


def far_sends(parts, axis):
    return (shift(parts[3], axis, 1), shift(parts[4], axis, -1))


def side_sends(parts, pair, axis):
    own, below, above = parts[:3]
    half = pair[0].shape[0]
    above = above.at[:half].set(total((above[:half], pair[0])))
    below = below.at[half:].set(total((below[half:], pair[1])))
    return (own, shift(above, axis, 1), shift(below, axis, -1))


def params():
    return pltpu.CompilerParams(vmem_limit_bytes=VMEM)


def cost(flops, nbytes):
    return pl.CostEstimate(flops=int(flops), bytes_accessed=int(nbytes), transcendentals=0)


def piece(refs, outer, inner, rows):
    if outer < 3:
        return refs[outer], inner * rows
    return refs[3 + inner // 2], (inner % 2) * rows


def pair_blocks(refs, p, rows):
    left, right = [], []
    for h in range(2):
        y, x = p // 2, (p % 2) * 2 + h
        ref, first = piece(refs[:5], y, x, rows)
        left.append(ref[first : first + 128, :])
        ref, first = piece(refs[5:], x, y, 128)
        right.append(ref[first : first + 128, :])
    return jnp.concatenate(left, 0), jnp.concatenate(right, 0)


def make_tables(base, refs, slot_ref, gate_ref):
    row = lax.broadcasted_iota(jnp.int32, (256, 256), 0)
    col = lax.broadcasted_iota(jnp.int32, (256, 256), 1)
    before = jnp.where((row < col) & ((row < 128) == (col < 128)), 1.0, 0.0).astype(BF16)
    lane = lax.broadcasted_iota(jnp.int32, (RING, 256), 1)
    index = lax.broadcasted_iota(jnp.int32, (RING, 256), 0)
    for p in range(PAIRS):
        both = []
        for h in range(2):
            ref, first = piece(refs[:5], p // 2, (p % 2) * 2 + h, BLOCK)
            both.append(ref[first + 128 : first + BLOCK, :256].astype(F32))
        ids = jnp.concatenate([t[:8, :128] for t in both], 1).astype(jnp.int32)
        gates = jnp.concatenate([t[8:, :128] + t[:8, 128:] + t[8:, 128:] for t in both], 1)
        chosen, weight = [], []
        for j in range(RING):
            match = ids == base + j * DEVS
            chosen.append(jnp.sum(jnp.where(match, 1.0, 0.0), axis=0, keepdims=True))
            weight.append(jnp.sum(jnp.where(match, gates, 0.0), axis=0, keepdims=True))
        chosen = jnp.concatenate(chosen, 0)
        place = jnp.dot(chosen.astype(BF16), before, preferred_element_type=F32)
        slot = place.astype(jnp.int32) + jnp.where(lane < 128, 0, CAP) + index * (2 * CAP)
        slot_ref[p] = jnp.where(chosen > 0.5, slot, -1)
        gate_ref[p] = jnp.concatenate(weight, 0)


def spread(slot, values):
    row = lax.broadcasted_iota(jnp.int32, (SLOTS, 256), 0)
    total = jnp.zeros((SLOTS, 256), F32)
    for j in range(RING):
        value = 1.0 if values is None else values[j : j + 1, :]
        total = jnp.where(slot[j : j + 1, :] == row, value, total)
    return total


def put_rows(out_ref, p, left, right):
    width = left.shape[1]
    for j in range(RING):
        rows = slice(p * 2 * CAP, (p + 1) * 2 * CAP)
        part = slice(j * 2 * CAP, (j + 1) * 2 * CAP)
        out_ref[j, rows, :width] = left[part]
        out_ref[j, rows, width:] = right[part]


def whole(*shape):
    return pl.BlockSpec(shape, lambda i: (0,) * len(shape))


def first_then(*shape):
    return pl.BlockSpec((1,) + shape, lambda i: (jnp.maximum(i - 1, 0),) + (0,) * len(shape))


def then_last(*shape):
    return pl.BlockSpec(
        (1,) + shape, lambda i: (jnp.minimum(i, RING - 1),) + (0,) * len(shape)
    )


def forward_kernel(base_ref, *refs):
    pieces, w_ref = refs[:10], refs[10]
    rows_ref, slot_ref, gate_ref, hidden_ref, factor_ref, held = refs[11:]
    step = pl.program_id(0)

    @pl.when(step == 0)
    def _():
        make_tables(base_ref[0], pieces, slot_ref, gate_ref)
        for p in range(PAIRS):
            onehot = spread(slot_ref[p], None).astype(BF16)
            left, right = (
                jnp.dot(onehot, block, preferred_element_type=F32).astype(BF16)
                for block in pair_blocks(pieces, p, BLOCK)
            )
            put_rows(held, p, left, right)

    @pl.when(step > 0)
    def _():
        rows = held[step - 1]
        rows_ref[0] = rows
        pre = jnp.dot(rows, w_ref[0], preferred_element_type=F32)
        inner = pre.shape[1] // 2
        gate, up = pre[:, :inner], pre[:, inner:]
        sig = jax.nn.sigmoid(gate)
        silu = gate * sig
        hidden_ref[0] = (silu * up).astype(BF16)
        factor_ref[0, :, :inner] = up * sig * (1.0 + gate * (1.0 - sig))
        factor_ref[0, :, inner:] = silu


def forward(base, pieces, w_gu):
    width, two = w_gu.shape[1:]
    cap = DEVS * CAP
    table = (PAIRS, RING, 256)
    return pl.pallas_call(
        forward_kernel,
        grid=(RING + 1,),
        out_shape=(
            jax.ShapeDtypeStruct((RING, cap, width), BF16),
            jax.ShapeDtypeStruct(table, jnp.int32),
            jax.ShapeDtypeStruct(table, F32),
            jax.ShapeDtypeStruct((RING, cap, two // 2), BF16),
            jax.ShapeDtypeStruct((RING, cap, two), F32),
        ),
        in_specs=[pl.BlockSpec(memory_space=pltpu.SMEM)]
        + [whole(*p.shape) for p in pieces]
        + [first_then(width, two)],
        out_specs=(
            first_then(cap, width),
            whole(*table),
            whole(*table),
            first_then(cap, two // 2),
            first_then(cap, two),
        ),
        scratch_shapes=[pltpu.VMEM((RING, cap, width), BF16)],
        name="forward",
        compiler_params=params(),
        cost_estimate=cost(11e9, 40e6),
    )(base, *pieces, w_gu)


def cot_kernel(slot_ref, gate_ref, *refs):
    pieces, hidden_ref, rows_ref, down_ref, held = refs[:10], *refs[10:]
    step = pl.program_id(0)

    @pl.when(step == 0)
    def _():
        for p in range(PAIRS):
            slot = slot_ref[p]
            onehot = spread(slot, None).astype(BF16)
            weight = jnp.sum(spread(slot, gate_ref[p]), axis=1, keepdims=True)
            left, right = (
                (jnp.dot(onehot, block, preferred_element_type=F32) * weight).astype(BF16)
                for block in pair_blocks(pieces, p, 128)
            )
            put_rows(held, p, left, right)

    @pl.when(step > 0)
    def _():
        rows = held[step - 1]
        rows_ref[0] = rows
        dims = (((0,), (0,)), ((), ()))
        out = lax.dot_general(hidden_ref[0], rows, dims, preferred_element_type=F32)
        out = out.astype(BF16)
        half = out.shape[1] // 2
        down_ref[0, 0] = out[:, :half]
        down_ref[0, 1] = out[:, half:]


def take_cot(slot, gate, pieces, hidden):
    width = 2 * pieces[0].shape[1]
    cap, inner = hidden.shape[1:]
    table = (PAIRS, RING, 256)
    return pl.pallas_call(
        cot_kernel,
        grid=(RING + 1,),
        out_shape=(
            jax.ShapeDtypeStruct((RING, cap, width), BF16),
            jax.ShapeDtypeStruct((RING, 2, inner, width // 2), BF16),
        ),
        in_specs=[whole(*table)] * 2
        + [whole(*p.shape) for p in pieces]
        + [first_then(cap, inner)],
        out_specs=(first_then(cap, width), first_then(2, inner, width // 2)),
        scratch_shapes=[pltpu.VMEM((RING, cap, width), BF16)],
        name="take_cot",
        compiler_params=params(),
        cost_estimate=cost(6e9, 22e6),
    )(slot, gate, *pieces, hidden)


def parts_of(width):
    big, small = (RING * 128, width), (RING * 64, width)
    return ((big,) * 3 + (small,) * 2) * 2


def give_rows(weighted, slot_ref, gate_ref, held, refs):
    width = held.shape[2] // 2
    dims = (((0,), (0,)), ((), ()))
    for p in range(PAIRS):
        slot = slot_ref[p]
        rows = held[:, p * 2 * CAP : (p + 1) * 2 * CAP, :].reshape(SLOTS, 2 * width)
        if weighted:
            weight = spread(slot, gate_ref[p])
            high = weight.astype(BF16)
            low = (weight - high.astype(F32)).astype(BF16)
            out = lax.dot_general(high, rows, dims, preferred_element_type=F32)
            out = out + lax.dot_general(low, rows, dims, preferred_element_type=F32)
        else:
            onehot = spread(slot, None).astype(BF16)
            out = lax.dot_general(onehot, rows, dims, preferred_element_type=F32)
        out = out.astype(BF16)
        for h in range(2):
            y, x = p // 2, (p % 2) * 2 + h
            block = out[h * 128 : (h + 1) * 128]
            ref, first = piece(refs[:5], y, x, 128)
            ref[first : first + 128, :] = block[:, :width]
            ref, first = piece(refs[5:], x, y, 128)
            ref[first : first + 128, :] = block[:, width:]


def out_kernel(slot_ref, gate_ref, hidden_ref, w_ref, *refs):
    step = pl.program_id(0)
    held = refs[10]

    @pl.when(step < RING)
    def _():
        out = jnp.dot(hidden_ref[0], w_ref[0], preferred_element_type=F32)
        held[step] = out.astype(BF16)

    @pl.when(step == RING)
    def _():
        give_rows(True, slot_ref, gate_ref, held, refs[:10])


def give_out(slot, gate, hidden, w_down):
    cap, inner = hidden.shape[1:]
    width = w_down.shape[2]
    table = (PAIRS, RING, 256)
    parts = parts_of(width // 2)
    return pl.pallas_call(
        out_kernel,
        grid=(RING + 1,),
        out_shape=tuple(jax.ShapeDtypeStruct(part, BF16) for part in parts),
        in_specs=[whole(*table)] * 2 + [then_last(cap, inner), then_last(inner, width)],
        out_specs=tuple(whole(*part) for part in parts),
        scratch_shapes=[pltpu.VMEM((RING, cap, width), BF16)],
        name="give_out",
        compiler_params=params(),
        cost_estimate=cost(9e9, 20e6),
    )(slot, gate, hidden, w_down)


def back_kernel(slot_ref, gate_ref, cot_ref, w_down_ref, factor_ref, w_gu_ref, *refs):
    step = pl.program_id(0)
    grad_ref, held = refs[10], refs[11]
    dims = (((1,), (1,)), ((), ()))

    @pl.when(step < RING)
    def _():
        hidden_grad = lax.dot_general(
            cot_ref[0], w_down_ref[0], dims, preferred_element_type=F32
        )
        inner = hidden_grad.shape[1]
        gate_grad = (hidden_grad * factor_ref[0, :, :inner]).astype(BF16)
        up_grad = (hidden_grad * factor_ref[0, :, inner:]).astype(BF16)
        both = jnp.concatenate([gate_grad, up_grad], 1)
        grad_ref[0] = both
        row = lax.dot_general(both, w_gu_ref[0], dims, preferred_element_type=F32)
        held[step] = row.astype(BF16)

    @pl.when(step == RING)
    def _():
        give_rows(False, slot_ref, gate_ref, held, refs[:10])


def give_back(slot, gate, cot_rows, w_down, factor, w_gu):
    cap, width = cot_rows.shape[1:]
    inner = w_down.shape[1]
    table = (PAIRS, RING, 256)
    parts = parts_of(width // 2)
    out = pl.pallas_call(
        back_kernel,
        grid=(RING + 1,),
        out_shape=tuple(jax.ShapeDtypeStruct(part, BF16) for part in parts)
        + (jax.ShapeDtypeStruct((RING, cap, 2 * inner), BF16),),
        in_specs=[whole(*table)] * 2
        + [
            then_last(cap, width),
            then_last(inner, width),
            then_last(cap, 2 * inner),
            then_last(width, 2 * inner),
        ],
        out_specs=tuple(whole(*part) for part in parts) + (then_last(cap, 2 * inner),),
        scratch_shapes=[pltpu.VMEM((RING, cap, width), BF16)],
        name="give_back",
        compiler_params=params(),
        cost_estimate=cost(15e9, 45e6),
    )(slot, gate, cot_rows, w_down, factor, w_gu)
    return out[:10], out[10]


def per_expert(*shape):
    return pl.BlockSpec((1,) + shape, lambda e: (e,) + (0,) * len(shape))


def outer_up_kernel(rows_ref, grad_ref, out_ref):
    dims = (((0,), (0,)), ((), ()))
    total = lax.dot_general(rows_ref[0], grad_ref[0], dims, preferred_element_type=F32)
    out_ref[0] = total.astype(BF16)


def outer_up(rows, grad):
    count, cap, width = rows.shape
    two = grad.shape[2]
    return pl.pallas_call(
        outer_up_kernel,
        grid=(count,),
        out_shape=jax.ShapeDtypeStruct((count, width, two), BF16),
        in_specs=[per_expert(cap, width), per_expert(cap, two)],
        out_specs=per_expert(width, two),
        name="outer_up",
        compiler_params=params(),
        cost_estimate=cost(8e9, 22e6),
    )(rows, grad)


def local(tokens, cotangent, expert_ids, gates, w_gate, w_up, w_down):
    width, inner = w_gate.shape[1:]
    half = width // 2
    core = lax.axis_index("edata")
    gate_half = lax.dynamic_slice_in_dim(w_gate[0], core * half, half, 0)
    up_half = lax.dynamic_slice_in_dim(w_up[0], core * half, half, 0)
    down_half = lax.dynamic_slice_in_dim(w_down[0], core * (inner // 2), inner // 2, 0)
    w_gu = lax.all_gather(
        jnp.concatenate([gate_half, up_half], 1), ("z", "edata"), axis=0, tiled=True
    ).reshape(RING, width, 2 * inner)
    w_dn = lax.all_gather(down_half, ("z", "edata"), axis=0, tiled=True).reshape(
        RING, inner, width
    )

    hi = lax.reduce_precision(gates.T, 8, 7)
    mid = lax.reduce_precision(gates.T - hi, 8, 7)
    ids = expert_ids.T.astype(F32)
    left = jnp.concatenate([ids, hi], 0)
    right = jnp.concatenate([mid, gates.T - hi - mid], 0)
    table = jnp.concatenate([left, right], 1).astype(BF16)
    table = jnp.pad(table, ((0, 0), (0, half - table.shape[1])))
    near_1 = near(jnp.concatenate([tokens[:, :half], table, cotangent[:, :half]], 0), "x")
    near_2 = near(jnp.concatenate([tokens[:, half:], cotangent[:, half:]], 0), "y")
    near_1, near_2 = together(near_1, near_2)
    tok_1 = jnp.concatenate([block[:BLOCK] for block in near_1], 0)
    tok_2 = jnp.concatenate([block[:128] for block in near_2], 0)
    cot_1 = jnp.concatenate([block[BLOCK:] for block in near_1], 0)
    cot_2 = jnp.concatenate([block[128:] for block in near_2], 0)

    side_1, side_2 = sides(tok_1, "y"), sides(tok_2, "x")
    side_1, side_2, (cot_1, cot_2) = together(side_1, side_2, (cot_1, cot_2))
    far_1, far_2 = fars(side_1, "y"), fars(side_2, "x")
    tok = (tok_1,) + side_1 + far_1 + (tok_2,) + side_2 + far_2

    base = lax.axis_index("y") * RING + lax.axis_index("x")
    rows, slot, gate, hidden, factor = forward(base.reshape(1).astype(jnp.int32), tok, w_gu)
    side_1, side_2 = sides(cot_1, "y"), sides(cot_2, "x")
    side_1, side_2, (rows, slot, gate, hidden, factor) = together(
        side_1, side_2, (rows, slot, gate, hidden, factor)
    )
    far_1, far_2 = fars(side_1, "y"), fars(side_2, "x")
    cot = (cot_1,) + side_1 + far_1 + (cot_2,) + side_2 + far_2

    out = give_out(slot, gate, hidden, w_dn)
    out_1, out_2 = out[:5], out[5:]
    far_1, far_2 = far_sends(out_1, "y"), far_sends(out_2, "x")
    cot_rows, down = take_cot(after(slot, *out), gate, cot, hidden)
    far_1, far_2, (cot_rows, down) = together(far_1, far_2, (cot_rows, down))
    down = down.reshape(2 * RING * inner, half)
    down_sum = lax.psum_scatter(down, ("z", "edata"), scatter_dimension=0, tiled=True)

    side_1, side_2 = side_sends(out_1, far_1, "y"), side_sends(out_2, far_2, "x")
    gin, grad = give_back(slot, gate, cot_rows, w_dn, factor, w_gu)
    side_1, side_2, gin, (grad,) = together(side_1, side_2, gin, (grad,))

    gin_1, gin_2 = gin[:5], gin[5:]
    far_1, far_2 = far_sends(gin_1, "y"), far_sends(gin_2, "x")
    both = outer_up(rows, grad).reshape(RING * width, 2 * inner)
    both_sum = lax.psum_scatter(both, ("z", "edata"), scatter_dimension=0, tiled=True)
    out_1, out_2 = cut(side_1), cut(side_2)

    side_1, side_2 = side_sends(gin_1, far_1, "y"), side_sends(gin_2, far_2, "x")
    side_1, side_2, (down_sum,) = together(side_1, side_2, (down_sum.astype(F32),))
    pairs_1 = [jnp.concatenate(pair, 0) for pair in zip(out_1, cut(side_1))]
    pairs_2 = [jnp.concatenate(pair, 0) for pair in zip(out_2, cut(side_2))]
    last_1, last_2 = sends(pairs_1, "x"), sends(pairs_2, "y")
    count = tokens.shape[0]
    mixed = [total([part[:count] for part in last]) for last in (last_1, last_2)]
    input_grad = [total([part[count:] for part in last]) for last in (last_1, last_2)]

    both_sum = both_sum.astype(F32)
    return (
        jnp.concatenate(mixed, 1),
        jnp.concatenate(input_grad, 1),
        both_sum[None, :, :inner],
        both_sum[None, :, inner:],
        down_sum[None],
    )


def solution(mesh):
    grid = Mesh(mesh.devices.reshape(RING, RING, RING, 2), ("z", "y", "x", "edata"))
    expert = ("z", "y", "x")
    rows = P(expert + ("edata",), None)
    weight = P(expert, None, None)
    return jax.shard_map(
        local,
        mesh=grid,
        in_specs=(rows, rows, rows, rows, weight, weight, weight),
        out_specs=(
            rows,
            rows,
            P(expert, "edata", None),
            P(expert, "edata", None),
            P(expert, None, "edata"),
        ),
        check_vma=False,
    )
```

```python
import jax
import jax.numpy as jnp
from jax import lax
from jax.experimental import pallas as pl
from jax.experimental.pallas import tpu as pltpu
from jax.sharding import Mesh, PartitionSpec as P

RING = 4
DEVS = 16
PAIRS = 8
CAP = 24
SLOTS = RING * 2 * CAP
BLOCK = 144
VMEM = 42 << 20
F32, BF16 = jnp.float32, jnp.bfloat16


def shift(block, axis, by):
    return lax.ppermute(block, axis, [(i, (i + by) % RING) for i in range(RING)])


def after(value, *others):
    return lax.optimization_barrier((value,) + others)[0]


def near(block, axis):
    return (block, shift(block, axis, 1), shift(block, axis, -1), shift(block, axis, 2))


def together(*groups):
    flat = lax.optimization_barrier(tuple(x for group in groups for x in group))
    out, at = [], 0
    for group in groups:
        out.append(flat[at : at + len(group)])
        at += len(group)
    return out


def sides(whole, axis):
    return (shift(whole, axis, 1), shift(whole, axis, -1))


def fars(pair, axis):
    half = pair[0].shape[0] // 2
    return (shift(pair[0][:half], axis, 1), shift(pair[1][half:], axis, -1))


def sends(parts, axis):
    own, below, above, far = parts
    return (own, shift(above, axis, 1), shift(below, axis, -1), shift(far, axis, 2))


def total(parts):
    out = parts[0].astype(F32)
    for part in parts[1:]:
        out = out + part.astype(F32)
    return out.astype(BF16)


def cut(parts):
    rows = parts[0].shape[0] // RING
    return [total([part[i * rows : (i + 1) * rows] for part in parts]) for i in range(RING)]


def far_sends(parts, axis):
    return (shift(parts[3], axis, 1), shift(parts[4], axis, -1))


def side_sends(parts, pair, axis):
    own, below, above = parts[:3]
    half = pair[0].shape[0]
    above = jnp.concatenate([total((above[:half], pair[0])), above[half:]], 0)
    below = jnp.concatenate([below[:half], total((below[half:], pair[1]))], 0)
    return (own, shift(above, axis, 1), shift(below, axis, -1))


def params():
    return pltpu.CompilerParams(vmem_limit_bytes=VMEM)


def cost(flops, nbytes):
    return pl.CostEstimate(flops=int(flops), bytes_accessed=int(nbytes), transcendentals=0)


def piece(refs, outer, inner, rows):
    if outer < 3:
        return refs[outer], inner * rows
    return refs[3 + inner // 2], (inner % 2) * rows


def pair_blocks(refs, p, rows):
    left, right = [], []
    for h in range(2):
        y, x = p // 2, (p % 2) * 2 + h
        ref, first = piece(refs[:5], y, x, rows)
        left.append(ref[first : first + 128, :])
        ref, first = piece(refs[5:], x, y, 128)
        right.append(ref[first : first + 128, :])
    return jnp.concatenate(left, 0), jnp.concatenate(right, 0)


def make_tables(base, refs, slot_ref, gate_ref):
    row = lax.broadcasted_iota(jnp.int32, (256, 256), 0)
    col = lax.broadcasted_iota(jnp.int32, (256, 256), 1)
    before = jnp.where((row < col) & ((row < 128) == (col < 128)), 1.0, 0.0).astype(BF16)
    lane = lax.broadcasted_iota(jnp.int32, (RING, 256), 1)
    index = lax.broadcasted_iota(jnp.int32, (RING, 256), 0)
    for p in range(PAIRS):
        both = []
        for h in range(2):
            ref, first = piece(refs[:5], p // 2, (p % 2) * 2 + h, BLOCK)
            both.append(ref[first + 128 : first + BLOCK, :256].astype(F32))
        ids = jnp.concatenate([t[:8, :128] for t in both], 1).astype(jnp.int32)
        gates = jnp.concatenate([t[8:, :128] + t[:8, 128:] + t[8:, 128:] for t in both], 1)
        chosen, weight = [], []
        for j in range(RING):
            match = ids == base + j * DEVS
            chosen.append(jnp.sum(jnp.where(match, 1.0, 0.0), axis=0, keepdims=True))
            weight.append(jnp.sum(jnp.where(match, gates, 0.0), axis=0, keepdims=True))
        chosen = jnp.concatenate(chosen, 0)
        place = jnp.dot(chosen.astype(BF16), before, preferred_element_type=F32)
        slot = place.astype(jnp.int32) + jnp.where(lane < 128, 0, CAP) + index * (2 * CAP)
        slot_ref[p] = jnp.where(chosen > 0.5, slot, -1)
        gate_ref[p] = jnp.concatenate(weight, 0)


def spread(slot, values):
    row = lax.broadcasted_iota(jnp.int32, (SLOTS, 256), 0)
    total = jnp.zeros((SLOTS, 256), F32)
    for j in range(RING):
        value = 1.0 if values is None else values[j : j + 1, :]
        total = jnp.where(slot[j : j + 1, :] == row, value, total)
    return total


def put_rows(out_ref, p, left, right):
    width = left.shape[1]
    for j in range(RING):
        rows = slice(p * 2 * CAP, (p + 1) * 2 * CAP)
        part = slice(j * 2 * CAP, (j + 1) * 2 * CAP)
        out_ref[j, rows, :width] = left[part]
        out_ref[j, rows, width:] = right[part]


def whole(*shape):
    return pl.BlockSpec(shape, lambda i: (0,) * len(shape))


def first_then(*shape):
    return pl.BlockSpec((1,) + shape, lambda i: (jnp.maximum(i - 1, 0),) + (0,) * len(shape))


def then_last(*shape):
    return pl.BlockSpec(
        (1,) + shape, lambda i: (jnp.minimum(i, RING - 1),) + (0,) * len(shape)
    )


def forward_kernel(base_ref, *refs):
    pieces, w_ref = refs[:10], refs[10]
    rows_ref, slot_ref, gate_ref, hidden_ref, factor_ref, held = refs[11:]
    step = pl.program_id(0)

    @pl.when(step == 0)
    def _():
        make_tables(base_ref[0], pieces, slot_ref, gate_ref)
        for p in range(PAIRS):
            onehot = spread(slot_ref[p], None).astype(BF16)
            left, right = (
                jnp.dot(onehot, block, preferred_element_type=F32).astype(BF16)
                for block in pair_blocks(pieces, p, BLOCK)
            )
            put_rows(held, p, left, right)

    @pl.when(step > 0)
    def _():
        rows = held[step - 1]
        rows_ref[0] = rows
        pre = jnp.dot(rows, w_ref[0], preferred_element_type=F32)
        inner = pre.shape[1] // 2
        gate, up = pre[:, :inner], pre[:, inner:]
        sig = jax.nn.sigmoid(gate)
        silu = gate * sig
        hidden_ref[0] = (silu * up).astype(BF16)
        factor_ref[0, :, :inner] = up * sig * (1.0 + gate * (1.0 - sig))
        factor_ref[0, :, inner:] = silu


def forward(base, pieces, w_gu):
    width, two = w_gu.shape[1:]
    cap = DEVS * CAP
    table = (PAIRS, RING, 256)
    return pl.pallas_call(
        forward_kernel,
        grid=(RING + 1,),
        out_shape=(
            jax.ShapeDtypeStruct((RING, cap, width), BF16),
            jax.ShapeDtypeStruct(table, jnp.int32),
            jax.ShapeDtypeStruct(table, F32),
            jax.ShapeDtypeStruct((RING, cap, two // 2), BF16),
            jax.ShapeDtypeStruct((RING, cap, two), F32),
        ),
        in_specs=[pl.BlockSpec(memory_space=pltpu.SMEM)]
        + [whole(*p.shape) for p in pieces]
        + [first_then(width, two)],
        out_specs=(
            first_then(cap, width),
            whole(*table),
            whole(*table),
            first_then(cap, two // 2),
            first_then(cap, two),
        ),
        scratch_shapes=[pltpu.VMEM((RING, cap, width), BF16)],
        name="forward",
        compiler_params=params(),
        cost_estimate=cost(11e9, 40e6),
    )(base, *pieces, w_gu)


def cot_kernel(slot_ref, gate_ref, *refs):
    pieces, hidden_ref, rows_ref, down_ref, held = refs[:10], *refs[10:]
    step = pl.program_id(0)

    @pl.when(step == 0)
    def _():
        for p in range(PAIRS):
            slot = slot_ref[p]
            onehot = spread(slot, None).astype(BF16)
            weight = jnp.sum(spread(slot, gate_ref[p]), axis=1, keepdims=True)
            left, right = (
                (jnp.dot(onehot, block, preferred_element_type=F32) * weight).astype(BF16)
                for block in pair_blocks(pieces, p, 128)
            )
            put_rows(held, p, left, right)

    @pl.when(step > 0)
    def _():
        rows = held[step - 1]
        rows_ref[0] = rows
        dims = (((0,), (0,)), ((), ()))
        out = lax.dot_general(hidden_ref[0], rows, dims, preferred_element_type=F32)
        out = out.astype(BF16)
        half = out.shape[1] // 2
        down_ref[0, 0] = out[:, :half]
        down_ref[0, 1] = out[:, half:]


def take_cot(slot, gate, pieces, hidden):
    width = 2 * pieces[0].shape[1]
    cap, inner = hidden.shape[1:]
    table = (PAIRS, RING, 256)
    return pl.pallas_call(
        cot_kernel,
        grid=(RING + 1,),
        out_shape=(
            jax.ShapeDtypeStruct((RING, cap, width), BF16),
            jax.ShapeDtypeStruct((RING, 2, inner, width // 2), BF16),
        ),
        in_specs=[whole(*table)] * 2
        + [whole(*p.shape) for p in pieces]
        + [first_then(cap, inner)],
        out_specs=(first_then(cap, width), first_then(2, inner, width // 2)),
        scratch_shapes=[pltpu.VMEM((RING, cap, width), BF16)],
        name="take_cot",
        compiler_params=params(),
        cost_estimate=cost(6e9, 22e6),
    )(slot, gate, *pieces, hidden)


def parts_of(width):
    big, small = (RING * 128, width), (RING * 64, width)
    return ((big,) * 3 + (small,) * 2) * 2


def give_rows(weighted, slot_ref, gate_ref, held, refs):
    width = held.shape[2] // 2
    dims = (((0,), (0,)), ((), ()))
    for p in range(PAIRS):
        slot = slot_ref[p]
        rows = held[:, p * 2 * CAP : (p + 1) * 2 * CAP, :].reshape(SLOTS, 2 * width)
        if weighted:
            weight = spread(slot, gate_ref[p])
            high = weight.astype(BF16)
            low = (weight - high.astype(F32)).astype(BF16)
            out = lax.dot_general(high, rows, dims, preferred_element_type=F32)
            out = out + lax.dot_general(low, rows, dims, preferred_element_type=F32)
        else:
            onehot = spread(slot, None).astype(BF16)
            out = lax.dot_general(onehot, rows, dims, preferred_element_type=F32)
        out = out.astype(BF16)
        for h in range(2):
            y, x = p // 2, (p % 2) * 2 + h
            block = out[h * 128 : (h + 1) * 128]
            ref, first = piece(refs[:5], y, x, 128)
            ref[first : first + 128, :] = block[:, :width]
            ref, first = piece(refs[5:], x, y, 128)
            ref[first : first + 128, :] = block[:, width:]


def out_kernel(slot_ref, gate_ref, hidden_ref, w_ref, *refs):
    step = pl.program_id(0)
    held = refs[10]

    @pl.when(step < RING)
    def _():
        out = jnp.dot(hidden_ref[0], w_ref[0], preferred_element_type=F32)
        held[step] = out.astype(BF16)

    @pl.when(step == RING)
    def _():
        give_rows(True, slot_ref, gate_ref, held, refs[:10])


def give_out(slot, gate, hidden, w_down):
    cap, inner = hidden.shape[1:]
    width = w_down.shape[2]
    table = (PAIRS, RING, 256)
    parts = parts_of(width // 2)
    return pl.pallas_call(
        out_kernel,
        grid=(RING + 1,),
        out_shape=tuple(jax.ShapeDtypeStruct(part, BF16) for part in parts),
        in_specs=[whole(*table)] * 2 + [then_last(cap, inner), then_last(inner, width)],
        out_specs=tuple(whole(*part) for part in parts),
        scratch_shapes=[pltpu.VMEM((RING, cap, width), BF16)],
        name="give_out",
        compiler_params=params(),
        cost_estimate=cost(9e9, 20e6),
    )(slot, gate, hidden, w_down)


def back_kernel(slot_ref, gate_ref, cot_ref, w_down_ref, factor_ref, w_gu_ref, *refs):
    step = pl.program_id(0)
    grad_ref, held = refs[10], refs[11]
    dims = (((1,), (1,)), ((), ()))

    @pl.when(step < RING)
    def _():
        hidden_grad = lax.dot_general(
            cot_ref[0], w_down_ref[0], dims, preferred_element_type=F32
        )
        inner = hidden_grad.shape[1]
        gate_grad = (hidden_grad * factor_ref[0, :, :inner]).astype(BF16)
        up_grad = (hidden_grad * factor_ref[0, :, inner:]).astype(BF16)
        both = jnp.concatenate([gate_grad, up_grad], 1)
        grad_ref[0] = both
        row = lax.dot_general(both, w_gu_ref[0], dims, preferred_element_type=F32)
        held[step] = row.astype(BF16)

    @pl.when(step == RING)
    def _():
        give_rows(False, slot_ref, gate_ref, held, refs[:10])


def give_back(slot, gate, cot_rows, w_down, factor, w_gu):
    cap, width = cot_rows.shape[1:]
    inner = w_down.shape[1]
    table = (PAIRS, RING, 256)
    parts = parts_of(width // 2)
    out = pl.pallas_call(
        back_kernel,
        grid=(RING + 1,),
        out_shape=tuple(jax.ShapeDtypeStruct(part, BF16) for part in parts)
        + (jax.ShapeDtypeStruct((RING, cap, 2 * inner), BF16),),
        in_specs=[whole(*table)] * 2
        + [
            then_last(cap, width),
            then_last(inner, width),
            then_last(cap, 2 * inner),
            then_last(width, 2 * inner),
        ],
        out_specs=tuple(whole(*part) for part in parts) + (then_last(cap, 2 * inner),),
        scratch_shapes=[pltpu.VMEM((RING, cap, width), BF16)],
        name="give_back",
        compiler_params=params(),
        cost_estimate=cost(15e9, 45e6),
    )(slot, gate, cot_rows, w_down, factor, w_gu)
    return out[:10], out[10]


def per_expert(*shape):
    return pl.BlockSpec((1,) + shape, lambda e: (e,) + (0,) * len(shape))


def outer_up_kernel(rows_ref, grad_ref, out_ref):
    dims = (((0,), (0,)), ((), ()))
    total = lax.dot_general(rows_ref[0], grad_ref[0], dims, preferred_element_type=F32)
    out_ref[0] = total.astype(BF16)


def outer_up(rows, grad):
    count, cap, width = rows.shape
    two = grad.shape[2]
    return pl.pallas_call(
        outer_up_kernel,
        grid=(count,),
        out_shape=jax.ShapeDtypeStruct((count, width, two), BF16),
        in_specs=[per_expert(cap, width), per_expert(cap, two)],
        out_specs=per_expert(width, two),
        name="outer_up",
        compiler_params=params(),
        cost_estimate=cost(8e9, 22e6),
    )(rows, grad)


def local(tokens, cotangent, expert_ids, gates, w_gate, w_up, w_down):
    width, inner = w_gate.shape[1:]
    half = width // 2
    core = lax.axis_index("edata")
    gate_half = lax.dynamic_slice_in_dim(w_gate[0], core * half, half, 0)
    up_half = lax.dynamic_slice_in_dim(w_up[0], core * half, half, 0)
    down_half = lax.dynamic_slice_in_dim(w_down[0], core * (inner // 2), inner // 2, 0)
    w_gu = lax.all_gather(
        jnp.concatenate([gate_half, up_half], 1), ("z", "edata"), axis=0, tiled=True
    ).reshape(RING, width, 2 * inner)
    w_dn = lax.all_gather(down_half, ("z", "edata"), axis=0, tiled=True).reshape(
        RING, inner, width
    )

    hi = lax.reduce_precision(gates.T, 8, 7)
    mid = lax.reduce_precision(gates.T - hi, 8, 7)
    ids = expert_ids.T.astype(F32)
    left = jnp.concatenate([ids, hi], 0)
    right = jnp.concatenate([mid, gates.T - hi - mid], 0)
    table = jnp.concatenate([left, right], 1).astype(BF16)
    table = jnp.pad(table, ((0, 0), (0, half - table.shape[1])))
    near_1 = near(jnp.concatenate([tokens[:, :half], table, cotangent[:, :half]], 0), "x")
    near_2 = near(jnp.concatenate([tokens[:, half:], cotangent[:, half:]], 0), "y")
    near_1, near_2 = together(near_1, near_2)
    tok_1 = jnp.concatenate([block[:BLOCK] for block in near_1], 0)
    tok_2 = jnp.concatenate([block[:128] for block in near_2], 0)
    cot_1 = jnp.concatenate([block[BLOCK:] for block in near_1], 0)
    cot_2 = jnp.concatenate([block[128:] for block in near_2], 0)

    side_1, side_2 = sides(tok_1, "y"), sides(tok_2, "x")
    side_1, side_2, (cot_1, cot_2) = together(side_1, side_2, (cot_1, cot_2))
    far_1, far_2 = fars(side_1, "y"), fars(side_2, "x")
    tok = (tok_1,) + side_1 + far_1 + (tok_2,) + side_2 + far_2

    base = lax.axis_index("y") * RING + lax.axis_index("x")
    rows, slot, gate, hidden, factor = forward(base.reshape(1).astype(jnp.int32), tok, w_gu)
    side_1, side_2 = sides(cot_1, "y"), sides(cot_2, "x")
    side_1, side_2, (rows, slot, gate, hidden, factor) = together(
        side_1, side_2, (rows, slot, gate, hidden, factor)
    )
    far_1, far_2 = fars(side_1, "y"), fars(side_2, "x")
    cot = (cot_1,) + side_1 + far_1 + (cot_2,) + side_2 + far_2

    out = give_out(slot, gate, hidden, w_dn)
    out_1, out_2 = out[:5], out[5:]
    far_1, far_2 = far_sends(out_1, "y"), far_sends(out_2, "x")
    cot_rows, down = take_cot(after(slot, *out), gate, cot, hidden)
    far_1, far_2, (cot_rows, down) = together(far_1, far_2, (cot_rows, down))
    down = down.reshape(2 * RING * inner, half)
    down_sum = lax.psum_scatter(down, ("z", "edata"), scatter_dimension=0, tiled=True)

    side_1, side_2 = side_sends(out_1, far_1, "y"), side_sends(out_2, far_2, "x")
    gin, grad = give_back(slot, gate, cot_rows, w_dn, factor, w_gu)
    side_1, side_2, gin, (grad,) = together(side_1, side_2, gin, (grad,))

    gin_1, gin_2 = gin[:5], gin[5:]
    far_1, far_2 = far_sends(gin_1, "y"), far_sends(gin_2, "x")
    near_1, near_2 = sends(cut(side_1), "x"), sends(cut(side_2), "y")
    both = outer_up(rows, grad).reshape(RING * width, 2 * inner)
    both_sum = lax.psum_scatter(both, ("z", "edata"), scatter_dimension=0, tiled=True)
    near_1, near_2, far_1, far_2, (down_sum,) = together(
        near_1, near_2, far_1, far_2, (down_sum.astype(F32),)
    )

    side_1, side_2 = side_sends(gin_1, far_1, "y"), side_sends(gin_2, far_2, "x")
    last_1, last_2 = sends(cut(side_1), "x"), sends(cut(side_2), "y")
    mixed = jnp.concatenate([total(near_1), total(near_2)], 1)
    input_grad = jnp.concatenate([total(last_1), total(last_2)], 1)

    both_sum = both_sum.astype(F32)
    return (
        mixed,
        input_grad,
        both_sum[None, :, :inner],
        both_sum[None, :, inner:],
        down_sum[None],
    )


def solution(mesh):
    grid = Mesh(mesh.devices.reshape(RING, RING, RING, 2), ("z", "y", "x", "edata"))
    expert = ("z", "y", "x")
    rows = P(expert + ("edata",), None)
    weight = P(expert, None, None)
    return jax.shard_map(
        local,
        mesh=grid,
        in_specs=(rows, rows, rows, rows, weight, weight, weight),
        out_specs=(
            rows,
            rows,
            P(expert, "edata", None),
            P(expert, "edata", None),
            P(expert, None, "edata"),
        ),
        check_vma=False,
    )
```
